256 devices in a mesh: ctx: 64 (over x_lo, y, z), head: 4 (over x_hi, core).
Axes of the slice: x: 4 (x_hi: 2, x_lo: 2; x = x_hi * 2 + x_lo), y: 4, z: 8, core: 2. Of those that a mesh axis runs over, the one named last changes fastest.
Arguments:
- queries: bfloat16 [64, 3, 256, 2048], P('ctx', None, None, 'head'), may hold values from -5 to 5
- keys: bfloat16 [64, 3, 256, 2048], P('ctx', None, None, 'head'), may hold values from -5 to 5
- values: bfloat16 [64, 3, 256, 2048], P('ctx', None, None, 'head'), may hold values from -6 to 6
- grad_out: bfloat16 [64, 3, 256, 2048], P('ctx', None, 'head'), may hold values from -6 to 6
- window_start: int32 [64, 3], replicated, may hold values from 0 to 61, as said below
- key_counts: int32 [64, 3], replicated, may hold values from 64 to 256, as said below
Outputs:
- attended: bfloat16 [64, 3, 256, 2048], P('ctx', None, None, 'head')
- grad_queries: bfloat16 [64, 3, 256, 2048], P('ctx', None, None, 'head')
- grad_keys: bfloat16 [64, 3, 256, 2048], P('ctx', None, None, 'head')
- grad_values: bfloat16 [64, 3, 256, 2048], P('ctx', None, None, 'head')
The draws below stay inside these ranges and needn't reach their ends.
Inputs may be any that keep to these rules, and one draw needn't show every extreme that they name: window_start[c, t] = clip(c - r, 0, 61) with r one of 0 to 2. `key_counts`: only tiles of the last of the 3 time tiles hold fewer than 256 live tokens.
All inputs are finite; a program needn't handle non-finite values.
Results may differ from the reference program's by a relative error of at most 0.011.
Values may be sent and summed in bfloat16 or wider, within the bound.
A program may use at most 128 MiB of HBM per device.

```python
import jax
import jax.numpy as jnp
from jax import lax

HEADS = 16
DH = 128
WIN = 3
TT = 3
COLS = 64
TILE = 256


def draw_queries(key, part):
    key = jax.random.fold_in(key, 1)
    base = jax.random.truncated_normal(key, -5.0, 5.0, (COLS, TT, TILE, HEADS, DH), jnp.float32)
    return base.reshape(COLS, TT, TILE, HEADS * DH).astype(jnp.bfloat16)


def draw_keys(key, part):
    key = jax.random.fold_in(key, 2)
    base = jax.random.truncated_normal(key, -5.0, 5.0, (COLS, TT, TILE, HEADS, DH), jnp.float32)
    return base.reshape(COLS, TT, TILE, HEADS * DH).astype(jnp.bfloat16)


def draw_window_start(key, part):
    key = jax.random.fold_in(key, 11)
    places = jnp.arange(COLS, dtype=jnp.int32)[:, None] + jnp.zeros((1, TT), jnp.int32)
    back = jax.random.randint(key, (COLS, TT), 0, WIN)
    back = back.at[WIN - 1, 0].set(WIN - 1)
    return jnp.clip(places - back, 0, COLS - WIN).astype(jnp.int32)


def draw_key_counts(key, part):
    key = jax.random.fold_in(key, 23)
    padded = jax.random.randint(key, (COLS, TT), TILE // 4, TILE + 1)
    padded = padded.at[0, TT - 1].set(TILE // 4)
    later = jnp.arange(TT, dtype=jnp.int32)[None, :] + jnp.zeros((COLS, 1), jnp.int32)
    return jnp.where(later == TT - 1, padded, TILE).astype(jnp.int32)


def steps_of(key, dims, split, low, top_value):
    def one(dim, shards_of):
        steps = jax.random.uniform(jax.random.fold_in(jax.random.fold_in(key, 6), dim), (shards_of,), jnp.float32, low / len(split), top_value / len(split))
        return jnp.repeat(jnp.exp(steps), dims[dim] // shards_of).reshape((-1,) + (1,) * (len(dims) - dim - 1))

    gain = one(*split[0])
    for cut in split[1:]:
        gain = gain * one(*cut)
    return gain


def noise(stream_key, shape, spread, limit, shards=(), kind=jnp.bfloat16):
    array = jax.random.normal(stream_key, shape, jnp.float32) * spread
    if len(shards) > 0:
        array = steps_of(stream_key, shape, shards, -0.22, 0.18) * array
    return jnp.clip(array, min=-limit, max=limit).astype(kind)


def setup_inputs(seed: int = 0) -> dict:
    splits = jax.random.split(jax.random.key(seed), 7)
    return {
        "queries": draw_queries(jax.random.fold_in(splits[6], 71), 0),
        "keys": draw_keys(jax.random.fold_in(splits[6], 71), 0),
        "values": noise(splits[2], (COLS, TT, TILE, HEADS * DH), 1.0, 6.0, ((0, 64), (3, 4))),
        "grad_out": noise(splits[3], (COLS, TT, TILE, HEADS * DH), 1.0, 6.0, ((0, 64), (2, 4))),
        "window_start": draw_window_start(jax.random.fold_in(splits[6], 71), 0),
        "key_counts": draw_key_counts(jax.random.fold_in(splits[6], 71), 0),
    }


def tile_core(query, grad, key_block, value_block, live):
    factor = DH ** -0.5
    query32 = query.astype(jnp.float32)
    grad32 = grad.astype(jnp.float32)
    keys32 = key_block.astype(jnp.float32)
    values32 = value_block.astype(jnp.float32)
    scores = jnp.einsum("qhd,khd->hqk", query32, keys32) * factor
    scores = jnp.where(live[None, None, :], scores, -jnp.inf)
    row_max = jnp.max(scores, axis=-1, keepdims=True)
    total = jnp.sum(jnp.exp(scores - row_max), axis=-1, keepdims=True)
    log_total = row_max + jnp.log(total)
    probs = jnp.exp(scores - log_total)
    weights = probs.astype(jnp.bfloat16)
    weights32 = weights.astype(jnp.float32)
    attended = jnp.einsum("hqk,khd->qhd", weights32, values32).astype(jnp.bfloat16)
    delta = jnp.sum(grad32 * attended.astype(jnp.float32), axis=-1).T
    dprobs = jnp.einsum("qhd,khd->hqk", grad32, values32)
    dscores = (probs * (dprobs - delta[:, :, None])).astype(jnp.bfloat16)
    dscores32 = dscores.astype(jnp.float32)
    grad_query = (jnp.einsum("hqk,khd->qhd", dscores32, keys32) * factor).astype(jnp.bfloat16)
    key_part = jnp.einsum("hqk,qhd->khd", dscores32, query32) * factor
    value_part = jnp.einsum("hqk,qhd->khd", weights32, grad32)
    return attended, grad_query, key_part, value_part


def reference(queries, keys, values, grad_out, window_start, key_counts):
    times, columns, tile_len, width = queries.shape
    head_count = width // DH
    breadth = min(WIN, columns)
    window_keys = WIN * breadth * tile_len
    positions = jnp.arange(tile_len, dtype=jnp.int32)
    zero = jnp.zeros((), jnp.int32)

    def visit(carry, index):
        key_sum, value_sum = carry
        time_tile = (index // columns).astype(jnp.int32)
        column = (index % columns).astype(jnp.int32)
        first_time = window_start[time_tile, column].astype(jnp.int32)
        first_col = jnp.clip(column - 1, 0, columns - breadth).astype(jnp.int32)
        start = (first_time, first_col, zero, zero)
        shape = (WIN, breadth, tile_len, width)
        key_block = lax.dynamic_slice(keys, start, shape).reshape(window_keys, head_count, DH)
        value_block = lax.dynamic_slice(values, start, shape).reshape(window_keys, head_count, DH)
        counts = lax.dynamic_slice(key_counts, (first_time, first_col), (WIN, breadth))
        live = (positions[None, None, :] < counts[:, :, None]).reshape(window_keys)
        own = (time_tile, column, zero, zero)
        query = lax.dynamic_slice(queries, own, (1, 1, tile_len, width)).reshape(tile_len, head_count, DH)
        grad = lax.dynamic_slice(grad_out, own, (1, 1, tile_len, width)).reshape(tile_len, head_count, DH)
        attended, grad_query, key_part, value_part = tile_core(query, grad, key_block, value_block, live)
        key_sum = lax.dynamic_update_slice(key_sum, lax.dynamic_slice(key_sum, start, shape) + key_part.reshape(shape), start)
        value_sum = lax.dynamic_update_slice(value_sum, lax.dynamic_slice(value_sum, start, shape) + value_part.reshape(shape), start)
        return (key_sum, value_sum), (attended.reshape(tile_len, width), grad_query.reshape(tile_len, width))

    empty = jnp.zeros((times, columns, tile_len, width), jnp.float32)
    sums, outputs = lax.scan(visit, (empty, empty), jnp.arange(times * columns, dtype=jnp.int32))
    attended = outputs[0].reshape(times, columns, tile_len, width)
    grad_queries = outputs[1].reshape(times, columns, tile_len, width)
    return attended, grad_queries, sums[0].astype(jnp.bfloat16), sums[1].astype(jnp.bfloat16)
```

```python
import functools

import jax
import jax.numpy as jnp
from jax import lax
from jax.experimental import pallas as pl
from jax.experimental.pallas import tpu as pltpu
from jax.sharding import PartitionSpec as P

DH = 128
WIN = 3
SLOTS = 2 * WIN - 1
OWN = WIN - 1
SCALE = DH ** (-0.5)
LOG2E = 1.4426950408889634
MESH = pl.DeviceIdType.MESH
F32 = jnp.float32
BF16 = jnp.bfloat16

NT = (((1,), (1,)), ((), ()))


def dot_nt(a, b):
    return lax.dot_general(a, b, NT, preferred_element_type=F32)


def dot_nn(a, b):
    return jnp.dot(a, b, preferred_element_type=F32)


def fold(block, op):
    rows, lanes = block.shape
    return op(block.reshape(rows // 8, 8, lanes), axis=0)


def kernel(
    heads,
    times,
    tile,
    groups,
    start_ref,
    count_ref,
    q_hbm,
    k_hbm,
    v_hbm,
    g_hbm,
    att_hbm,
    dq_hbm,
    dk_hbm,
    dv_hbm,
    kv,
    far_out,
    far_in,
    near_out,
    near_in,
    near_sum,
    own_sum,
    q_buf,
    g_buf,
    att_buf,
    dq_buf,
    dk_buf,
    dv_buf,
    k_cur,
    v_cur,
    kt_cur,
    vt_cur,
    s_buf,
    dp_buf,
    w_buf,
    ds_buf,
    load_sem,
    g_here,
    g_send,
    g_recv,
    own_send,
    own_recv,
    relay_send,
    relay_recv,
    far_send,
    far_recv,
    near_send,
    near_recv,
    out_sem,
):
    count = lax.axis_size("ctx")
    here = lax.axis_index("ctx")
    group = lax.axis_index("head")
    left = lax.rem(here + count - 1, count)
    right = lax.rem(here + 1, count)
    toward = (left, right)
    part = tile // groups
    chunks = WIN * times

    def lanes(head):
        return pl.ds(pl.multiple_of(head * DH, DH), DH)

    def load(which, head):
        source, target = (
            (k_hbm, kv.at[head, OWN, 0]),
            (v_hbm, kv.at[head, OWN, 1]),
            (q_hbm, q_buf.at[head]),
        )[which]
        return pltpu.make_async_copy(
            source.at[:, :, lanes(head)], target, load_sem.at[head, which]
        )

    def remote(source, target, sends, recvs, head, side):
        return pltpu.make_async_remote_copy(
            src_ref=source,
            dst_ref=target,
            send_sem=sends.at[head, side],
            recv_sem=recvs.at[head, side],
            device_id=(toward[side], group),
            device_id_type=MESH,
        )

    def own_copy(head, side):
        slot = OWN + 1 if side == 0 else OWN - 1
        return remote(kv.at[head, OWN], kv.at[head, slot], own_send, own_recv, head, side)

    def relay_copy(head, side):
        slot = OWN + 1 if side == 0 else OWN - 1
        target = OWN + 2 if side == 0 else OWN - 2
        return remote(kv.at[head, slot], kv.at[head, target], relay_send, relay_recv, head, side)

    def far_copy(head, side):
        return remote(
            far_out.at[head, side], far_in.at[head, side], far_send, far_recv, head, side
        )

    def near_copy(head, side):
        return remote(
            near_out.at[head, side], near_in.at[head, side], near_send, near_recv, head, side
        )

    def grad_copy(step, head):
        peer = lax.rem(group + step, groups)
        return pltpu.make_async_remote_copy(
            src_ref=g_hbm.at[:, :, lanes(peer * heads + head)],
            dst_ref=g_buf.at[head, :, pl.ds(pl.multiple_of(group * part, part), part), :],
            send_sem=g_send.at[step, head],
            recv_sem=g_recv.at[step, head],
            device_id=(here, peer),
            device_id_type=MESH,
        )

    def grad_here(head):
        return pltpu.make_async_copy(
            g_hbm.at[:, :, lanes(group * heads + head)],
            g_buf.at[head, :, pl.ds(pl.multiple_of(group * part, part), part), :],
            g_here.at[head],
        )

    def out_copy(which, head):
        source, target = (
            (att_buf, att_hbm),
            (dq_buf, dq_hbm),
            (dk_buf, dk_hbm),
            (dv_buf, dv_hbm),
        )[which]
        return pltpu.make_async_copy(
            source.at[head], target.at[:, :, lanes(head)], out_sem.at[which, head]
        )

    for head in range(heads):
        for which in range(3):
            load(which, head).start()
    for head in range(heads):
        grad_here(head).start()

    barrier = pltpu.get_barrier_semaphore()
    for neighbour in toward:
        pl.semaphore_signal(barrier, inc=1, device_id=(neighbour, group), device_id_type=MESH)
    for step in range(1, groups):
        pl.semaphore_signal(
            barrier,
            inc=1,
            device_id=(here, lax.rem(group + step, groups)),
            device_id_type=MESH,
        )
    pl.semaphore_wait(barrier, 2 + groups - 1)

    def send_own(head):
        load(0, head).wait()
        load(1, head).wait()
        for side in range(2):
            own_copy(head, side).start()

    def send_relay(head):
        for side in (1, 0):
            own_copy(head, side).wait_recv()
            relay_copy(head, side).start()

    send_own(0)
    for step in range(1, groups):
        grad_copy(step, 0).start()
    send_own(1)
    for head in range(1, heads):
        for step in range(1, groups):
            grad_copy(step, head).start()

    zero_tile = jnp.zeros((tile, tile), BF16)
    for t in range(times):
        for j in range(times):
            w_buf[t, WIN, j] = zero_tile
            ds_buf[t, WIN, j] = zero_tile
    row = lax.broadcasted_iota(jnp.int32, (tile, tile), 0)

    send_relay(0)
    if heads > 2:
        send_own(2)
    send_relay(1)
    for head in range(3, heads):
        send_own(head)

    def tile_step(head, t):
        start = jnp.clip(start_ref[here, t], 0, count - WIN)
        rel = jnp.clip(start - here + OWN, 0, OWN)
        q = q_buf[head, t]
        g = g_buf[head, t]

        def place(i):
            return i // times, i % times

        def scores(i, top):
            s, j = place(i)
            block = dot_nt(k_cur[rel + s, j], q) * (SCALE * LOG2E)
            block = jnp.where(row < count_ref[start + s, j], block, -jnp.inf)
            s_buf[i] = block
            return jnp.maximum(top, fold(block, jnp.max))

        top = lax.fori_loop(0, chunks, scores, jnp.full((8, tile), -jnp.inf, F32))
        top = jnp.max(top, axis=0, keepdims=True)

        def exps(i, total):
            s, j = place(i)
            block = jnp.exp2(s_buf[i] - top)
            s_buf[i] = block
            dp_buf[i] = dot_nt(v_cur[rel + s, j], g)
            return total + fold(block, jnp.sum)

        total = lax.fori_loop(0, chunks, exps, jnp.zeros((8, tile), F32))
        inverse = 1.0 / jnp.sum(total, axis=0, keepdims=True)

        def attend(i, att):
            s, j = place(i)
            probs = s_buf[i] * inverse
            s_buf[i] = probs
            weights = probs.astype(BF16)
            w_buf[t, s, j] = weights
            return att + dot_nn(vt_cur[rel + s, j], weights)

        att = lax.fori_loop(0, chunks, attend, jnp.zeros((DH, tile), F32))
        rounded = att.astype(BF16).astype(F32)
        att_buf[head, t] = rounded.T.astype(BF16)
        delta = jnp.sum(g.astype(F32).T * rounded, axis=0, keepdims=True)

        def back(i, dq):
            s, j = place(i)
            dscores = (s_buf[i] * (dp_buf[i] - delta)).astype(BF16)
            ds_buf[t, s, j] = dscores
            return dq + dot_nn(kt_cur[rel + s, j], dscores)

        dq = lax.fori_loop(0, chunks, back, jnp.zeros((DH, tile), F32))
        dq_buf[head, t] = (dq * SCALE).T.astype(BF16)

    def key_side(head):
        rels = [jnp.clip(start_ref[here, t] - here + OWN, 0, OWN) for t in range(times)]

        def parts(slot, j):
            dk = jnp.zeros((tile, DH), F32)
            dv = jnp.zeros((tile, DH), F32)
            for t in range(times):
                s = slot - rels[t]
                s = jnp.where((s >= 0) & (s < WIN), s, WIN)
                dk = dk + dot_nn(ds_buf[t, s, j], q_buf[head, t])
                dv = dv + dot_nn(w_buf[t, s, j], g_buf[head, t])
            return dk * SCALE, dv

        for slot in (0, SLOTS - 1, 1, SLOTS - 2, OWN):

            def one(j, carry, slot=slot):
                pair = parts(slot, j)
                for which in range(2):
                    if slot == 0:
                        far_out[head, 0, which, j] = pair[which].astype(BF16)
                    elif slot == SLOTS - 1:
                        far_out[head, 1, which, j] = pair[which].astype(BF16)
                    elif slot == OWN:
                        own_sum[head, which, j] = pair[which]
                    else:
                        near_sum[head, 0 if slot < OWN else 1, which, j] = pair[which]
                return carry

            lax.fori_loop(0, times, one, 0)
            if slot in (0, SLOTS - 1):
                side = 0 if slot == 0 else 1

                @pl.when(head > 0)
                def _():
                    far_copy(head, side).start()

    def send_near(head):
        for side in range(2):
            far_copy(head, side).wait_recv()
            for which in range(2):

                def one(j, carry, which=which, side=side):
                    near_out[head, side, which, j] = (
                        near_sum[head, side, which, j]
                        + far_in[head, side, which, j].astype(F32)
                    ).astype(BF16)
                    return carry

                lax.fori_loop(0, times, one, 0)
            near_copy(head, side).start()

    def finish(head):
        for side in range(2):
            near_copy(head, side).wait_recv()

        def one(j, carry):
            for which, out in enumerate((dk_buf, dv_buf)):
                out[head, j] = (
                    own_sum[head, which, j]
                    + near_in[head, 0, which, j].astype(F32)
                    + near_in[head, 1, which, j].astype(F32)
                ).astype(BF16)
            return carry

        lax.fori_loop(0, times, one, 0)
        out_copy(2, head).start()
        out_copy(3, head).start()

    def head_step(head, carry):
        load(2, head).wait()
        grad_here(head).wait()
        for step in range(1, groups):
            grad_copy(step, head).wait_recv()
        for side in range(2):
            relay_copy(head, side).wait_recv()

        def stage(i, inner):
            slot, j = i // times, i % times
            keys = kv[head, slot, 0, j]
            values = kv[head, slot, 1, j]
            k_cur[slot, j] = keys
            v_cur[slot, j] = values
            kt_cur[slot, j] = keys.T
            vt_cur[slot, j] = values.T
            return inner

        lax.fori_loop(0, SLOTS * times, stage, 0)

        def visit(t, inner):
            tile_step(head, t)
            return inner

        lax.fori_loop(0, times, visit, 0)
        out_copy(0, head).start()
        out_copy(1, head).start()
        key_side(head)

        @pl.when(head == 0)
        def _():
            for later in range(2, heads):
                send_relay(later)
            for side in range(2):
                far_copy(head, side).start()

        @pl.when(head > 0)
        def _():
            send_near(head - 1)

        @pl.when(head > 1)
        def _():
            finish(head - 2)

        return carry

    lax.fori_loop(0, heads, head_step, 0)
    send_near(heads - 1)
    finish(heads - 2)
    finish(heads - 1)

    def drain(head, carry):
        for side in range(2):
            own_copy(head, side).wait_send()
            relay_copy(head, side).wait_send()
            far_copy(head, side).wait_send()
            near_copy(head, side).wait_send()
        for step in range(1, groups):
            grad_copy(step, head).wait_send()
        for which in range(4):
            out_copy(which, head).wait()
        return carry

    lax.fori_loop(0, heads, drain, 0)


def shards(queries, keys, values, grad_out, window_start, key_counts):
    _, times, tile, width = queries.shape
    heads = width // DH
    groups = tile // grad_out.shape[2]
    block = (times, tile, DH)
    dma = pltpu.SemaphoreType.DMA
    any_spec = pl.BlockSpec(memory_space=pl.ANY)
    smem_spec = pl.BlockSpec(memory_space=pltpu.SMEM)
    out = jax.ShapeDtypeStruct((times, tile, width), BF16)
    pairs = times * heads * 6 * tile * WIN * times * tile * DH * 2
    results = pl.pallas_call(
        functools.partial(kernel, heads, times, tile, groups),
        out_shape=(out,) * 4,
        in_specs=[smem_spec, smem_spec] + [any_spec] * 4,
        out_specs=(any_spec,) * 4,
        scratch_shapes=[
            pltpu.VMEM((heads, SLOTS, 2) + block, BF16),
            pltpu.VMEM((heads, 2, 2) + block, BF16),
            pltpu.VMEM((heads, 2, 2) + block, BF16),
            pltpu.VMEM((heads, 2, 2) + block, BF16),
            pltpu.VMEM((heads, 2, 2) + block, BF16),
            pltpu.VMEM((heads, 2, 2) + block, F32),
            pltpu.VMEM((heads, 2) + block, F32),
            pltpu.VMEM((heads,) + block, BF16),
            pltpu.VMEM((heads,) + block, BF16),
            pltpu.VMEM((heads,) + block, BF16),
            pltpu.VMEM((heads,) + block, BF16),
            pltpu.VMEM((heads,) + block, BF16),
            pltpu.VMEM((heads,) + block, BF16),
            pltpu.VMEM((SLOTS, times, tile, DH), BF16),
            pltpu.VMEM((SLOTS, times, tile, DH), BF16),
            pltpu.VMEM((SLOTS, times, DH, tile), BF16),
            pltpu.VMEM((SLOTS, times, DH, tile), BF16),
            pltpu.VMEM((WIN * times, tile, tile), F32),
            pltpu.VMEM((WIN * times, tile, tile), F32),
            pltpu.VMEM((times, WIN + 1, times, tile, tile), BF16),
            pltpu.VMEM((times, WIN + 1, times, tile, tile), BF16),
            dma((heads, 3)),
            dma((heads,)),
            dma((groups, heads)),
            dma((groups, heads)),
            dma((heads, 2)),
            dma((heads, 2)),
            dma((heads, 2)),
            dma((heads, 2)),
            dma((heads, 2)),
            dma((heads, 2)),
            dma((heads, 2)),
            dma((heads, 2)),
            dma((4, heads)),
        ],
        compiler_params=pltpu.CompilerParams(
            collective_id=0, has_side_effects=True, vmem_limit_bytes=60 * 1024 * 1024
        ),
        cost_estimate=pl.CostEstimate(
            flops=pairs, bytes_accessed=8 * times * tile * width * 2, transcendentals=0
        ),
        name="band_attention",
    )(window_start, key_counts, queries[0], keys[0], values[0], grad_out[0])
    return tuple(result[None] for result in results)


def solution(mesh):
    placed = (
        P("ctx", None, None, "head"),
        P("ctx", None, None, "head"),
        P("ctx", None, None, "head"),
        P("ctx", None, "head", None),
        P(),
        P(),
    )
    return jax.shard_map(
        shards,
        mesh=mesh,
        in_specs=placed,
        out_specs=(P("ctx", None, None, "head"),) * 4,
        check_vma=False,
    )
```

```python
import functools

import jax
import jax.numpy as jnp
from jax import lax
from jax.experimental import pallas as pl
from jax.experimental.pallas import tpu as pltpu
from jax.sharding import PartitionSpec as P

DH = 128
WIN = 3
SLOTS = 2 * WIN - 1
OWN = WIN - 1
SCALE = DH ** (-0.5)
LOG2E = 1.4426950408889634
MESH = pl.DeviceIdType.MESH
F32 = jnp.float32
BF16 = jnp.bfloat16

NT = (((1,), (1,)), ((), ()))


def dot_nt(a, b):
    return lax.dot_general(a, b, NT, preferred_element_type=F32)


def dot_nn(a, b):
    return jnp.dot(a, b, preferred_element_type=F32)


def looped(unroll, count, body, carry):
    return lax.fori_loop(0, count, body, carry, unroll=unroll)


def fold(block, op):
    rows, lanes = block.shape
    return op(block.reshape(rows // 8, 8, lanes), axis=0)


def kernel(
    heads,
    times,
    tile,
    groups,
    start_ref,
    count_ref,
    q_hbm,
    k_hbm,
    v_hbm,
    g_hbm,
    att_hbm,
    dq_hbm,
    dk_hbm,
    dv_hbm,
    kv,
    far_out,
    far_in,
    near_out,
    near_in,
    near_sum,
    own_sum,
    q_buf,
    g_buf,
    att_buf,
    dq_buf,
    dk_buf,
    dv_buf,
    k_cur,
    v_cur,
    kt_cur,
    vt_cur,
    s_buf,
    dp_buf,
    w_buf,
    ds_buf,
    load_sem,
    g_here,
    g_send,
    g_recv,
    own_send,
    own_recv,
    relay_send,
    relay_recv,
    far_send,
    far_recv,
    near_send,
    near_recv,
    out_sem,
):
    count = lax.axis_size("ctx")
    here = lax.axis_index("ctx")
    group = lax.axis_index("head")
    left = lax.rem(here + count - 1, count)
    right = lax.rem(here + 1, count)
    toward = (left, right)
    part = tile // groups
    chunks = WIN * times
    width = heads * DH

    def lanes(head):
        return pl.ds(pl.multiple_of(head * DH, DH), DH)

    def load(which, head):
        source, target = (
            (k_hbm, kv.at[head, OWN, 0]),
            (v_hbm, kv.at[head, OWN, 1]),
            (q_hbm, q_buf.at[head]),
        )[which]
        return pltpu.make_async_copy(
            source.at[:, :, lanes(head)], target, load_sem.at[head, which]
        )

    def remote(source, target, sends, recvs, head, side):
        return pltpu.make_async_remote_copy(
            src_ref=source,
            dst_ref=target,
            send_sem=sends.at[head, side],
            recv_sem=recvs.at[head, side],
            device_id=(toward[side], group),
            device_id_type=MESH,
        )

    def own_copy(head, side):
        slot = OWN + 1 if side == 0 else OWN - 1
        return remote(kv.at[head, OWN], kv.at[head, slot], own_send, own_recv, head, side)

    def relay_copy(head, side):
        slot = OWN + 1 if side == 0 else OWN - 1
        target = OWN + 2 if side == 0 else OWN - 2
        return remote(kv.at[head, slot], kv.at[head, target], relay_send, relay_recv, head, side)

    def far_copy(head, side):
        return remote(
            far_out.at[head, side], far_in.at[head, side], far_send, far_recv, head, side
        )

    def near_copy(head, side):
        return remote(
            near_out.at[head, side], near_in.at[head, side], near_send, near_recv, head, side
        )

    def grad_rows():
        return g_buf.at[:, pl.ds(pl.multiple_of(group * part, part), part), :]

    def grad_lanes(owner):
        return g_hbm.at[:, :, pl.ds(pl.multiple_of(owner * width, width), width)]

    def grad_copy(step):
        peer = lax.rem(group + step, groups)
        return pltpu.make_async_remote_copy(
            src_ref=grad_lanes(peer),
            dst_ref=grad_rows(),
            send_sem=g_send.at[step],
            recv_sem=g_recv.at[step],
            device_id=(here, peer),
            device_id_type=MESH,
        )

    def grad_here():
        return pltpu.make_async_copy(grad_lanes(group), grad_rows(), g_here)

    def out_copy(which, head):
        source, target = (
            (att_buf, att_hbm),
            (dq_buf, dq_hbm),
            (dk_buf, dk_hbm),
            (dv_buf, dv_hbm),
        )[which]
        return pltpu.make_async_copy(
            source.at[head], target.at[:, :, lanes(head)], out_sem.at[which, head]
        )

    for head in range(heads):
        for which in range(3):
            load(which, head).start()
    grad_here().start()

    barrier = pltpu.get_barrier_semaphore()
    for neighbour in toward:
        pl.semaphore_signal(barrier, inc=1, device_id=(neighbour, group), device_id_type=MESH)
    for step in range(1, groups):
        pl.semaphore_signal(
            barrier,
            inc=1,
            device_id=(here, lax.rem(group + step, groups)),
            device_id_type=MESH,
        )
    pl.semaphore_wait(barrier, 2 + groups - 1)

    def send_own(head):
        load(0, head).wait()
        load(1, head).wait()
        for side in range(2):
            own_copy(head, side).start()

    def send_relay(head):
        for side in (1, 0):
            own_copy(head, side).wait_recv()
            relay_copy(head, side).start()

    for step in range(1, groups):
        grad_copy(step).start()
    grad_here().wait()
    for step in range(1, groups):
        grad_copy(step).wait_recv()
    send_own(0)
    send_own(1)

    zero_tile = jnp.zeros((tile, tile), BF16)
    for t in range(times):
        for j in range(times):
            w_buf[t, WIN, j] = zero_tile
            ds_buf[t, WIN, j] = zero_tile
    row = lax.broadcasted_iota(jnp.int32, (tile, tile), 0)

    send_relay(0)
    if heads > 2:
        send_own(2)
    send_relay(1)
    for head in range(3, heads):
        send_own(head)

    def tile_step(head, t):
        start = jnp.clip(start_ref[here, t], 0, count - WIN)
        rel = jnp.clip(start - here + OWN, 0, OWN)
        q = q_buf[head, t]
        g = g_buf[t, :, lanes(head)]

        def place(i):
            return i // times, i % times

        def scores(i, top):
            s, j = place(i)
            block = dot_nt(k_cur[rel + s, j], q) * (SCALE * LOG2E)
            block = jnp.where(row < count_ref[start + s, j], block, -jnp.inf)
            s_buf[i] = block
            return jnp.maximum(top, fold(block, jnp.max))

        top = looped(9, chunks, scores, jnp.full((8, tile), -jnp.inf, F32))
        top = jnp.max(top, axis=0, keepdims=True)

        def exps(i, total):
            s, j = place(i)
            block = jnp.exp2(s_buf[i] - top)
            s_buf[i] = block
            dp_buf[i] = dot_nt(v_cur[rel + s, j], g)
            return total + fold(block, jnp.sum)

        total = looped(9, chunks, exps, jnp.zeros((8, tile), F32))
        inverse = 1.0 / jnp.sum(total, axis=0, keepdims=True)

        def attend(i, att):
            s, j = place(i)
            probs = s_buf[i] * inverse
            s_buf[i] = probs
            weights = probs.astype(BF16)
            w_buf[t, s, j] = weights
            return att + dot_nn(vt_cur[rel + s, j], weights)

        att = looped(9, chunks, attend, jnp.zeros((DH, tile), F32))
        rounded = att.astype(BF16).astype(F32)
        att_buf[head, t] = rounded.T.astype(BF16)
        delta = jnp.sum(g.astype(F32).T * rounded, axis=0, keepdims=True)

        def back(i, dq):
            s, j = place(i)
            dscores = (s_buf[i] * (dp_buf[i] - delta)).astype(BF16)
            ds_buf[t, s, j] = dscores
            return dq + dot_nn(kt_cur[rel + s, j], dscores)

        dq = looped(9, chunks, back, jnp.zeros((DH, tile), F32))
        dq_buf[head, t] = (dq * SCALE).T.astype(BF16)

    def key_side(head):
        rels = [jnp.clip(start_ref[here, t] - here + OWN, 0, OWN) for t in range(times)]

        def parts(slot, j):
            dk = jnp.zeros((tile, DH), F32)
            dv = jnp.zeros((tile, DH), F32)
            for t in range(times):
                s = slot - rels[t]
                s = jnp.where((s >= 0) & (s < WIN), s, WIN)
                dk = dk + dot_nn(ds_buf[t, s, j], q_buf[head, t])
                dv = dv + dot_nn(w_buf[t, s, j], g_buf[t, :, lanes(head)])
            return dk * SCALE, dv

        for slot in (0, SLOTS - 1, 1, SLOTS - 2, OWN):

            def one(j, carry, slot=slot):
                pair = parts(slot, j)
                for which in range(2):
                    if slot == 0:
                        far_out[head, 0, which, j] = pair[which].astype(BF16)
                    elif slot == SLOTS - 1:
                        far_out[head, 1, which, j] = pair[which].astype(BF16)
                    elif slot == OWN:
                        own_sum[head, which, j] = pair[which]
                    else:
                        near_sum[head, 0 if slot < OWN else 1, which, j] = pair[which]
                return carry

            lax.fori_loop(0, times, one, 0, unroll=True)
            if slot in (0, SLOTS - 1):
                side = 0 if slot == 0 else 1

                @pl.when(head > 0)
                def _():
                    far_copy(head, side).start()

    def send_near(head):
        for side in range(2):
            far_copy(head, side).wait_recv()
            for which in range(2):

                def one(j, carry, which=which, side=side):
                    near_out[head, side, which, j] = (
                        near_sum[head, side, which, j]
                        + far_in[head, side, which, j].astype(F32)
                    ).astype(BF16)
                    return carry

                lax.fori_loop(0, times, one, 0)
            near_copy(head, side).start()

    def finish(head):
        for side in range(2):
            near_copy(head, side).wait_recv()

        def one(j, carry):
            for which, out in enumerate((dk_buf, dv_buf)):
                out[head, j] = (
                    own_sum[head, which, j]
                    + near_in[head, 0, which, j].astype(F32)
                    + near_in[head, 1, which, j].astype(F32)
                ).astype(BF16)
            return carry

        lax.fori_loop(0, times, one, 0)
        out_copy(2, head).start()
        out_copy(3, head).start()

    def head_step(head, carry):
        load(2, head).wait()

        for side in range(2):
            relay_copy(head, side).wait_recv()

        def stage(i, inner):
            slot, j = i // times, i % times
            keys = kv[head, slot, 0, j]
            values = kv[head, slot, 1, j]
            k_cur[slot, j] = keys
            v_cur[slot, j] = values
            kt_cur[slot, j] = keys.T
            vt_cur[slot, j] = values.T
            return inner

        lax.fori_loop(0, SLOTS * times, stage, 0)

        def visit(t, inner):
            tile_step(head, t)
            return inner

        lax.fori_loop(0, times, visit, 0)
        out_copy(0, head).start()
        out_copy(1, head).start()
        key_side(head)

        @pl.when(head == 0)
        def _():
            for later in range(2, heads):
                send_relay(later)
            for side in range(2):
                far_copy(head, side).start()

        @pl.when(head > 0)
        def _():
            send_near(head - 1)

        @pl.when(head > 1)
        def _():
            finish(head - 2)

        return carry

    lax.fori_loop(0, heads, head_step, 0)
    send_near(heads - 1)
    finish(heads - 2)
    finish(heads - 1)

    def drain(head, carry):
        for side in range(2):
            own_copy(head, side).wait_send()
            relay_copy(head, side).wait_send()
            far_copy(head, side).wait_send()
            near_copy(head, side).wait_send()
        for which in range(4):
            out_copy(which, head).wait()
        return carry

    lax.fori_loop(0, heads, drain, 0)
    for step in range(1, groups):
        grad_copy(step).wait_send()


def shards(queries, keys, values, grad_out, window_start, key_counts):
    _, times, tile, width = queries.shape
    heads = width // DH
    groups = tile // grad_out.shape[2]
    block = (times, tile, DH)
    dma = pltpu.SemaphoreType.DMA
    any_spec = pl.BlockSpec(memory_space=pl.ANY)
    smem_spec = pl.BlockSpec(memory_space=pltpu.SMEM)
    out = jax.ShapeDtypeStruct((times, tile, width), BF16)
    pairs = times * heads * 6 * tile * WIN * times * tile * DH * 2
    results = pl.pallas_call(
        functools.partial(kernel, heads, times, tile, groups),
        out_shape=(out,) * 4,
        in_specs=[smem_spec, smem_spec] + [any_spec] * 4,
        out_specs=(any_spec,) * 4,
        scratch_shapes=[
            pltpu.VMEM((heads, SLOTS, 2) + block, BF16),
            pltpu.VMEM((heads, 2, 2) + block, BF16),
            pltpu.VMEM((heads, 2, 2) + block, BF16),
            pltpu.VMEM((heads, 2, 2) + block, BF16),
            pltpu.VMEM((heads, 2, 2) + block, BF16),
            pltpu.VMEM((heads, 2, 2) + block, F32),
            pltpu.VMEM((heads, 2) + block, F32),
            pltpu.VMEM((heads,) + block, BF16),
            pltpu.VMEM((times, tile, width), BF16),
            pltpu.VMEM((heads,) + block, BF16),
            pltpu.VMEM((heads,) + block, BF16),
            pltpu.VMEM((heads,) + block, BF16),
            pltpu.VMEM((heads,) + block, BF16),
            pltpu.VMEM((SLOTS, times, tile, DH), BF16),
            pltpu.VMEM((SLOTS, times, tile, DH), BF16),
            pltpu.VMEM((SLOTS, times, DH, tile), BF16),
            pltpu.VMEM((SLOTS, times, DH, tile), BF16),
            pltpu.VMEM((WIN * times, tile, tile), F32),
            pltpu.VMEM((WIN * times, tile, tile), F32),
            pltpu.VMEM((times, WIN + 1, times, tile, tile), BF16),
            pltpu.VMEM((times, WIN + 1, times, tile, tile), BF16),
            dma((heads, 3)),
            dma,
            dma((groups,)),
            dma((groups,)),
            dma((heads, 2)),
            dma((heads, 2)),
            dma((heads, 2)),
            dma((heads, 2)),
            dma((heads, 2)),
            dma((heads, 2)),
            dma((heads, 2)),
            dma((heads, 2)),
            dma((4, heads)),
        ],
        compiler_params=pltpu.CompilerParams(
            collective_id=0, has_side_effects=True, vmem_limit_bytes=60 * 1024 * 1024
        ),
        cost_estimate=pl.CostEstimate(
            flops=pairs, bytes_accessed=8 * times * tile * width * 2, transcendentals=0
        ),
        name="band_attention",
    )(window_start, key_counts, queries[0], keys[0], values[0], grad_out[0])
    return tuple(result[None] for result in results)


def solution(mesh):
    placed = (
        P("ctx", None, None, "head"),
        P("ctx", None, None, "head"),
        P("ctx", None, None, "head"),
        P("ctx", None, "head", None),
        P(),
        P(),
    )
    return jax.shard_map(
        shards,
        mesh=mesh,
        in_specs=placed,
        out_specs=(P("ctx", None, None, "head"),) * 4,
        check_vma=False,
    )
```

```python
import functools

import jax
import jax.numpy as jnp
from jax import lax
from jax.experimental import pallas as pl
from jax.experimental.pallas import tpu as pltpu
from jax.sharding import PartitionSpec as P

DH = 128
WIN = 3
SLOTS = 2 * WIN - 1
OWN = WIN - 1
SCALE = DH ** (-0.5)
LOG2E = 1.4426950408889634
MESH = pl.DeviceIdType.MESH
F32 = jnp.float32
BF16 = jnp.bfloat16

NT = (((1,), (1,)), ((), ()))


def dot_nt(a, b):
    return lax.dot_general(a, b, NT, preferred_element_type=F32)


def dot_nn(a, b):
    return jnp.dot(a, b, preferred_element_type=F32)


def looped(unroll, count, body, carry):
    return lax.fori_loop(0, count, body, carry, unroll=unroll)


def fold(block, op):
    rows, lanes = block.shape
    return op(block.reshape(rows // 8, 8, lanes), axis=0)


def kernel(
    heads,
    times,
    tile,
    groups,
    start_ref,
    count_ref,
    q_hbm,
    k_hbm,
    v_hbm,
    g_hbm,
    att_hbm,
    dq_hbm,
    dk_hbm,
    dv_hbm,
    kv,
    far_out,
    far_in,
    near_out,
    near_in,
    near_sum,
    own_sum,
    q_buf,
    g_buf,
    att_buf,
    dq_buf,
    dk_buf,
    dv_buf,
    k_cur,
    v_cur,
    kt_cur,
    vt_cur,
    s_buf,
    dp_buf,
    w_buf,
    ds_buf,
    load_sem,
    g_here,
    g_send,
    g_recv,
    own_send,
    own_recv,
    relay_send,
    relay_recv,
    far_send,
    far_recv,
    near_send,
    near_recv,
    out_sem,
):
    count = lax.axis_size("ctx")
    here = lax.axis_index("ctx")
    group = lax.axis_index("head")
    left = lax.rem(here + count - 1, count)
    right = lax.rem(here + 1, count)
    toward = (left, right)
    part = tile // groups
    chunks = WIN * times
    width = heads * DH

    def lanes(head):
        return pl.ds(pl.multiple_of(head * DH, DH), DH)

    def load(which, head):
        source, target = (
            (k_hbm, kv.at[head, OWN, 0]),
            (v_hbm, kv.at[head, OWN, 1]),
            (q_hbm, q_buf.at[head]),
        )[which]
        return pltpu.make_async_copy(
            source.at[:, :, lanes(head)], target, load_sem.at[head, which]
        )

    def remote(source, target, sends, recvs, head, side):
        return pltpu.make_async_remote_copy(
            src_ref=source,
            dst_ref=target,
            send_sem=sends.at[head, side],
            recv_sem=recvs.at[head, side],
            device_id=(toward[side], group),
            device_id_type=MESH,
        )

    def own_copy(head, side):
        slot = OWN + 1 if side == 0 else OWN - 1
        return remote(kv.at[head, OWN], kv.at[head, slot], own_send, own_recv, head, side)

    def relay_copy(head, side):
        slot = OWN + 1 if side == 0 else OWN - 1
        target = OWN + 2 if side == 0 else OWN - 2
        return remote(kv.at[head, slot], kv.at[head, target], relay_send, relay_recv, head, side)

    def far_copy(head, side):
        return remote(
            far_out.at[head, side], far_in.at[head, side], far_send, far_recv, head, side
        )

    def near_copy(head, side):
        return remote(
            near_out.at[head, side], near_in.at[head, side], near_send, near_recv, head, side
        )

    def grad_rows():
        return g_buf.at[:, pl.ds(pl.multiple_of(group * part, part), part), :]

    def grad_lanes(owner):
        return g_hbm.at[:, :, pl.ds(pl.multiple_of(owner * width, width), width)]

    def grad_copy(step):
        peer = lax.rem(group + step, groups)
        return pltpu.make_async_remote_copy(
            src_ref=grad_lanes(peer),
            dst_ref=grad_rows(),
            send_sem=g_send.at[step],
            recv_sem=g_recv.at[step],
            device_id=(here, peer),
            device_id_type=MESH,
        )

    def grad_here():
        return pltpu.make_async_copy(grad_lanes(group), grad_rows(), g_here)

    def out_copy(which, head):
        source, target = (
            (att_buf, att_hbm),
            (dq_buf, dq_hbm),
            (dk_buf, dk_hbm),
            (dv_buf, dv_hbm),
        )[which]
        return pltpu.make_async_copy(
            source.at[head], target.at[:, :, lanes(head)], out_sem.at[which, head]
        )

    for head in range(heads):
        for which in range(3):
            load(which, head).start()
    grad_here().start()

    barrier = pltpu.get_barrier_semaphore()
    for neighbour in toward:
        pl.semaphore_signal(barrier, inc=1, device_id=(neighbour, group), device_id_type=MESH)
    for step in range(1, groups):
        pl.semaphore_signal(
            barrier,
            inc=1,
            device_id=(here, lax.rem(group + step, groups)),
            device_id_type=MESH,
        )
    pl.semaphore_wait(barrier, 2 + groups - 1)

    def send_own(head):
        load(0, head).wait()
        load(1, head).wait()
        for side in range(2):
            own_copy(head, side).start()

    def send_relay(head):
        for side in (1, 0):
            own_copy(head, side).wait_recv()
            relay_copy(head, side).start()

    for step in range(1, groups):
        grad_copy(step).start()
    grad_here().wait()
    for step in range(1, groups):
        grad_copy(step).wait_recv()
    send_own(0)
    send_own(1)

    zero_tile = jnp.zeros((tile, tile), BF16)
    for t in range(times):
        for j in range(times):
            w_buf[t, WIN, j] = zero_tile
            ds_buf[t, WIN, j] = zero_tile
    row = lax.broadcasted_iota(jnp.int32, (tile, tile), 0)

    send_relay(0)
    if heads > 2:
        send_own(2)
    send_relay(1)
    for head in range(3, heads):
        send_own(head)

    def tile_step(head, t):
        start = jnp.clip(start_ref[t, here], 0, count - WIN)
        rel = jnp.clip(start - here + OWN, 0, OWN)
        q = q_buf[head, t]
        g = g_buf[t, :, lanes(head)]

        def place(i):
            return i // times, i % times

        def scores(i, top):
            s, j = place(i)
            block = dot_nt(k_cur[rel + s, j], q) * (SCALE * LOG2E)
            block = jnp.where(row < count_ref[j, start + s], block, -jnp.inf)
            s_buf[i] = block
            return jnp.maximum(top, fold(block, jnp.max))

        top = looped(9, chunks, scores, jnp.full((8, tile), -jnp.inf, F32))
        top = jnp.max(top, axis=0, keepdims=True)

        def exps(i, total):
            s, j = place(i)
            block = jnp.exp2(s_buf[i] - top)
            s_buf[i] = block
            dp_buf[i] = dot_nt(v_cur[rel + s, j], g)
            return total + fold(block, jnp.sum)

        total = looped(9, chunks, exps, jnp.zeros((8, tile), F32))
        inverse = 1.0 / jnp.sum(total, axis=0, keepdims=True)

        def attend(i, att):
            s, j = place(i)
            probs = s_buf[i] * inverse
            s_buf[i] = probs
            weights = probs.astype(BF16)
            w_buf[t, s, j] = weights
            return att + dot_nn(vt_cur[rel + s, j], weights)

        att = looped(9, chunks, attend, jnp.zeros((DH, tile), F32))
        rounded = att.astype(BF16).astype(F32)
        att_buf[head, t] = rounded.T.astype(BF16)
        delta = jnp.sum(g.astype(F32).T * rounded, axis=0, keepdims=True)

        def back(i, dq):
            s, j = place(i)
            dscores = (s_buf[i] * (dp_buf[i] - delta)).astype(BF16)
            ds_buf[t, s, j] = dscores
            return dq + dot_nn(kt_cur[rel + s, j], dscores)

        dq = looped(9, chunks, back, jnp.zeros((DH, tile), F32))
        dq_buf[head, t] = (dq * SCALE).T.astype(BF16)

    def key_side(head):
        rels = [jnp.clip(start_ref[t, here] - here + OWN, 0, OWN) for t in range(times)]

        def parts(slot, j):
            dk = jnp.zeros((tile, DH), F32)
            dv = jnp.zeros((tile, DH), F32)
            for t in range(times):
                s = slot - rels[t]
                s = jnp.where((s >= 0) & (s < WIN), s, WIN)
                dk = dk + dot_nn(ds_buf[t, s, j], q_buf[head, t])
                dv = dv + dot_nn(w_buf[t, s, j], g_buf[t, :, lanes(head)])
            return dk * SCALE, dv

        for slot in (0, SLOTS - 1, 1, SLOTS - 2, OWN):

            def one(j, carry, slot=slot):
                pair = parts(slot, j)
                for which in range(2):
                    if slot == 0:
                        far_out[head, 0, which, j] = pair[which].astype(BF16)
                    elif slot == SLOTS - 1:
                        far_out[head, 1, which, j] = pair[which].astype(BF16)
                    elif slot == OWN:
                        own_sum[head, which, j] = pair[which]
                    else:
                        near_sum[head, 0 if slot < OWN else 1, which, j] = pair[which]
                return carry

            lax.fori_loop(0, times, one, 0, unroll=True)
            if slot in (0, SLOTS - 1):
                side = 0 if slot == 0 else 1

                @pl.when(head > 0)
                def _():
                    far_copy(head, side).start()

    def send_near(head):
        for side in range(2):
            far_copy(head, side).wait_recv()
            for which in range(2):

                def one(j, carry, which=which, side=side):
                    near_out[head, side, which, j] = (
                        near_sum[head, side, which, j]
                        + far_in[head, side, which, j].astype(F32)
                    ).astype(BF16)
                    return carry

                lax.fori_loop(0, times, one, 0)
            near_copy(head, side).start()

    def finish(head):
        for side in range(2):
            near_copy(head, side).wait_recv()

        def one(j, carry):
            for which, out in enumerate((dk_buf, dv_buf)):
                out[head, j] = (
                    own_sum[head, which, j]
                    + near_in[head, 0, which, j].astype(F32)
                    + near_in[head, 1, which, j].astype(F32)
                ).astype(BF16)
            return carry

        lax.fori_loop(0, times, one, 0)
        out_copy(2, head).start()
        out_copy(3, head).start()

    def head_step(head, carry):
        load(2, head).wait()

        for side in range(2):
            relay_copy(head, side).wait_recv()

        def stage(i, inner):
            slot, j = i // times, i % times
            keys = kv[head, slot, 0, j]
            values = kv[head, slot, 1, j]
            k_cur[slot, j] = keys
            v_cur[slot, j] = values
            kt_cur[slot, j] = keys.T
            vt_cur[slot, j] = values.T
            return inner

        lax.fori_loop(0, SLOTS * times, stage, 0)

        def visit(t, inner):
            tile_step(head, t)
            return inner

        lax.fori_loop(0, times, visit, 0)
        out_copy(0, head).start()
        out_copy(1, head).start()
        key_side(head)

        @pl.when(head == 0)
        def _():
            for later in range(2, heads):
                send_relay(later)
            for side in range(2):
                far_copy(head, side).start()

        @pl.when(head > 0)
        def _():
            send_near(head - 1)

        @pl.when(head > 1)
        def _():
            finish(head - 2)

        return carry

    lax.fori_loop(0, heads, head_step, 0)
    send_near(heads - 1)
    finish(heads - 2)
    finish(heads - 1)

    def drain(head, carry):
        for side in range(2):
            own_copy(head, side).wait_send()
            relay_copy(head, side).wait_send()
            far_copy(head, side).wait_send()
            near_copy(head, side).wait_send()
        for which in range(4):
            out_copy(which, head).wait()
        return carry

    lax.fori_loop(0, heads, drain, 0)
    for step in range(1, groups):
        grad_copy(step).wait_send()


def forward(times, *refs):
    sources, targets = refs[:4], refs[4:8]
    held, in_sem, out_sem = refs[8:]
    pieces = [(i, t) for t in range(times) for i in range(4)]
    inward = [
        pltpu.make_async_copy(sources[i].at[t], held.at[i, t], in_sem.at[i, t]) for i, t in pieces
    ]
    outward = [
        pltpu.make_async_copy(held.at[i, t], targets[i].at[t], out_sem.at[i, t]) for i, t in pieces
    ]
    for copy in inward:
        copy.start()
    for first, second in zip(inward, outward):
        first.wait()
        second.start()
    for copy in outward:
        copy.wait()


def shards(queries, keys, values, grad_out, window_start, key_counts):
    _, times, tile, width = queries.shape
    heads = width // DH
    groups = tile // grad_out.shape[2]
    block = (times, tile, DH)
    dma = pltpu.SemaphoreType.DMA
    any_spec = pl.BlockSpec(memory_space=pl.ANY)
    smem_spec = pl.BlockSpec(memory_space=pltpu.SMEM)
    out = jax.ShapeDtypeStruct((times, tile, width), BF16)
    pairs = times * heads * 6 * tile * WIN * times * tile * DH * 2
    results = pl.pallas_call(
        functools.partial(kernel, heads, times, tile, groups),
        out_shape=(out,) * 4,
        in_specs=[smem_spec, smem_spec] + [any_spec] * 4,
        out_specs=(any_spec,) * 4,
        scratch_shapes=[
            pltpu.VMEM((heads, SLOTS, 2) + block, BF16),
            pltpu.VMEM((heads, 2, 2) + block, BF16),
            pltpu.VMEM((heads, 2, 2) + block, BF16),
            pltpu.VMEM((heads, 2, 2) + block, BF16),
            pltpu.VMEM((heads, 2, 2) + block, BF16),
            pltpu.VMEM((heads, 2, 2) + block, F32),
            pltpu.VMEM((heads, 2) + block, F32),
            pltpu.VMEM((heads,) + block, BF16),
            pltpu.VMEM((times, tile, width), BF16),
            pltpu.VMEM((heads,) + block, BF16),
            pltpu.VMEM((heads,) + block, BF16),
            pltpu.VMEM((heads,) + block, BF16),
            pltpu.VMEM((heads,) + block, BF16),
            pltpu.VMEM((SLOTS, times, tile, DH), BF16),
            pltpu.VMEM((SLOTS, times, tile, DH), BF16),
            pltpu.VMEM((SLOTS, times, DH, tile), BF16),
            pltpu.VMEM((SLOTS, times, DH, tile), BF16),
            pltpu.VMEM((WIN * times, tile, tile), F32),
            pltpu.VMEM((WIN * times, tile, tile), F32),
            pltpu.VMEM((times, WIN + 1, times, tile, tile), BF16),
            pltpu.VMEM((times, WIN + 1, times, tile, tile), BF16),
            dma((heads, 3)),
            dma,
            dma((groups,)),
            dma((groups,)),
            dma((heads, 2)),
            dma((heads, 2)),
            dma((heads, 2)),
            dma((heads, 2)),
            dma((heads, 2)),
            dma((heads, 2)),
            dma((heads, 2)),
            dma((heads, 2)),
            dma((4, heads)),
        ],
        compiler_params=pltpu.CompilerParams(
            collective_id=0, has_side_effects=True, vmem_limit_bytes=60 * 1024 * 1024
        ),
        cost_estimate=pl.CostEstimate(
            flops=pairs, bytes_accessed=8 * times * tile * width * 2, transcendentals=0
        ),
        name="band_attention",
    )(window_start.T, key_counts.T, queries[0], keys[0], values[0], grad_out[0])
    results = pl.pallas_call(
        functools.partial(forward, times),
        out_shape=(out,) * 4,
        in_specs=[any_spec] * 4,
        out_specs=(any_spec,) * 4,
        scratch_shapes=[
            pltpu.VMEM((4, times, tile, width), BF16),
            dma((4, times)),
            dma((4, times)),
        ],
        name="place_results",
    )(*results)
    return tuple(result[None] for result in results)


def solution(mesh):
    placed = (
        P("ctx", None, None, "head"),
        P("ctx", None, None, "head"),
        P("ctx", None, None, "head"),
        P("ctx", None, "head", None),
        P(),
        P(),
    )
    return jax.shard_map(
        shards,
        mesh=mesh,
        in_specs=placed,
        out_specs=(P("ctx", None, None, "head"),) * 4,
        check_vma=False,
    )
```

```python
import functools

import jax
import jax.numpy as jnp
from jax import lax
from jax.experimental import pallas as pl
from jax.experimental.pallas import tpu as pltpu
from jax.sharding import PartitionSpec as P

DH = 128
WIN = 3
SLOTS = 2 * WIN - 1
OWN = WIN - 1
RUN = 8
SCALE = DH ** (-0.5)
LOG2E = 1.4426950408889634
MESH = pl.DeviceIdType.MESH
F32 = jnp.float32
BF16 = jnp.bfloat16

NT = (((1,), (1,)), ((), ()))


def dot_nt(a, b):
    return lax.dot_general(a, b, NT, preferred_element_type=F32)


def dot_nn(a, b):
    return jnp.dot(a, b, preferred_element_type=F32)


def looped(unroll, count, body, carry):
    return lax.fori_loop(0, count, body, carry, unroll=unroll)


def fold(block, op):
    rows, lanes = block.shape
    return op(block.reshape(rows // 8, 8, lanes), axis=0)


class Guarded:
    def __init__(self, copy, sends, receives):
        self.copy, self.sends, self.receives = copy, sends, receives

    def start(self):
        pl.when(self.sends)(lambda: self.copy.start())

    def wait_send(self):
        pl.when(self.sends)(lambda: self.copy.wait_send())

    def wait_recv(self):
        pl.when(self.receives)(lambda: self.copy.wait_recv())


def kernel(
    heads,
    times,
    tile,
    groups,
    start_ref,
    count_ref,
    q_hbm,
    k_hbm,
    v_hbm,
    g_hbm,
    att_hbm,
    dq_hbm,
    dk_hbm,
    dv_hbm,
    kv,
    far_out,
    far_in,
    near_out,
    near_in,
    near_sum,
    own_sum,
    q_buf,
    g_buf,
    att_buf,
    dq_buf,
    dk_buf,
    dv_buf,
    k_cur,
    v_cur,
    kt_cur,
    vt_cur,
    s_buf,
    dp_buf,
    w_buf,
    ds_buf,
    load_sem,
    g_here,
    chip_send,
    chip_recv,
    cross_send,
    cross_recv,
    half_send,
    half_recv,
    g_mid,
    own_send,
    own_recv,
    relay_send,
    relay_recv,
    far_send,
    far_recv,
    near_send,
    near_recv,
    out_sem,
):
    count = lax.axis_size("ctx")
    here = lax.axis_index("ctx")
    group = lax.axis_index("head")
    left = lax.rem(here + count - 1, count)
    right = lax.rem(here + 1, count)
    toward = (left, right)
    part = tile // groups
    chunks = WIN * times
    pair, core = group // 2, group % 2
    half = count // 2
    partner = lax.rem(here + half, count)
    flip = (here == half - RUN) | (here == half + RUN - 1)
    special = flip | (here == RUN - 1) | (here == count - RUN)
    next_pair = jnp.where(flip, 1 - pair, pair)
    width = heads * DH

    def lanes(head):
        return pl.ds(pl.multiple_of(head * DH, DH), DH)

    def load(which, head):
        source, target = (
            (k_hbm, kv.at[head, OWN, 0]),
            (v_hbm, kv.at[head, OWN, 1]),
            (q_hbm, q_buf.at[head]),
        )[which]
        return pltpu.make_async_copy(
            source.at[:, :, lanes(head)], target, load_sem.at[head, which]
        )

    def remote(source, target, sends, recvs, head, side):
        copy = pltpu.make_async_remote_copy(
            src_ref=source,
            dst_ref=target,
            send_sem=sends.at[head, side],
            recv_sem=recvs.at[head, side],
            device_id=(toward[side], group),
            device_id_type=MESH,
        )
        ends = (here > 0, here < count - 1)
        return Guarded(copy, ends[side], ends[1 - side])

    def own_copy(head, side):
        slot = OWN + 1 if side == 0 else OWN - 1
        return remote(kv.at[head, OWN], kv.at[head, slot], own_send, own_recv, head, side)

    def relay_copy(head, side):
        slot = OWN + 1 if side == 0 else OWN - 1
        target = OWN + 2 if side == 0 else OWN - 2
        return remote(kv.at[head, slot], kv.at[head, target], relay_send, relay_recv, head, side)

    def far_copy(head, side):
        return remote(
            far_out.at[head, side], far_in.at[head, side], far_send, far_recv, head, side
        )

    def near_copy(head, side):
        return remote(
            near_out.at[head, side], near_in.at[head, side], near_send, near_recv, head, side
        )

    def grad_rows(owner):
        return g_buf.at[:, pl.ds(pl.multiple_of(owner * part, part), part), :]

    def grad_lanes(owner):
        return g_hbm.at[:, :, pl.ds(pl.multiple_of(owner * width, width), width)]

    def grad_chip():
        peer = pair * 2 + 1 - core
        return pltpu.make_async_remote_copy(
            src_ref=grad_lanes(peer),
            dst_ref=grad_rows(group),
            send_sem=chip_send,
            recv_sem=chip_recv,
            device_id=(here, peer),
            device_id_type=MESH,
        )

    def grad_cross(other):
        peer = (1 - pair) * 2 + other
        return pltpu.make_async_remote_copy(
            src_ref=grad_lanes(peer),
            dst_ref=grad_rows(group),
            send_sem=cross_send.at[other],
            recv_sem=cross_recv.at[core],
            device_id=(here, peer),
            device_id_type=MESH,
        )

    def grad_half(other):
        return pltpu.make_async_remote_copy(
            src_ref=grad_lanes((1 - pair) * 2 + other),
            dst_ref=g_mid.at[other],
            send_sem=half_send.at[other],
            recv_sem=half_recv.at[other],
            device_id=(partner, next_pair * 2 + core),
            device_id_type=MESH,
        )

    def grad_onward(other):
        return pltpu.make_async_remote_copy(
            src_ref=g_mid.at[other],
            dst_ref=grad_rows((1 - next_pair) * 2 + core),
            send_sem=cross_send.at[other],
            recv_sem=cross_recv.at[core],
            device_id=(partner, next_pair * 2 + other),
            device_id_type=MESH,
        )

    def grad_arrival(other):
        return pltpu.make_async_remote_copy(
            src_ref=g_mid.at[other],
            dst_ref=grad_rows((1 - pair) * 2 + other),
            send_sem=cross_send.at[other],
            recv_sem=cross_recv.at[other],
            device_id=(here, (1 - pair) * 2 + other),
            device_id_type=MESH,
        )

    def grad_here():
        return pltpu.make_async_copy(grad_lanes(group), grad_rows(group), g_here)

    def out_copy(which, head):
        source, target = (
            (att_buf, att_hbm),
            (dq_buf, dq_hbm),
            (dk_buf, dk_hbm),
            (dv_buf, dv_hbm),
        )[which]
        return pltpu.make_async_copy(
            source.at[head], target.at[:, :, lanes(head)], out_sem.at[which, head]
        )

    for head in range(heads):
        for which in range(3):
            load(which, head).start()
    grad_here().start()

    barrier = pltpu.get_barrier_semaphore()
    for neighbour in toward:
        pl.semaphore_signal(barrier, inc=1, device_id=(neighbour, group), device_id_type=MESH)
    for step in range(1, groups):
        pl.semaphore_signal(
            barrier,
            inc=1,
            device_id=(here, lax.rem(group + step, groups)),
            device_id_type=MESH,
        )

    @pl.when(special)
    def _():
        for peer in range(groups):
            pl.semaphore_signal(barrier, inc=1, device_id=(partner, peer), device_id_type=MESH)

    pl.semaphore_wait(barrier, 2 + groups - 1 + jnp.where(special, groups, 0))

    zero_block = jnp.zeros(kv.shape[2:], BF16)
    for empty, side, slots in ((here == 0, 1, (0, 1)), (here == count - 1, 0, (3, 4))):

        @pl.when(empty)
        def _():
            def clear(head, carry):
                for slot in slots:
                    kv[head, slot] = zero_block
                far_in[head, side] = zero_block
                near_in[head, side] = zero_block
                return carry

            lax.fori_loop(0, heads, clear, 0)

    def send_own(head):
        load(0, head).wait()
        load(1, head).wait()
        for side in range(2):
            own_copy(head, side).start()

    def send_relay(head):
        for side in (1, 0):
            own_copy(head, side).wait_recv()
            relay_copy(head, side).start()

    grad_chip().start()

    @pl.when(special)
    def _():
        for other in range(2):
            grad_half(other).start()

    @pl.when(jnp.logical_not(special))
    def _():
        for other in range(2):
            grad_cross(other).start()

    send_own(0)
    send_own(1)

    @pl.when(special)
    def _():
        for other in range(2):
            grad_half(other).wait_recv()
            grad_onward(other).start()


    zero_tile = jnp.zeros((tile, tile), BF16)
    for t in range(times):
        for j in range(times):
            w_buf[t, WIN, j] = zero_tile
            ds_buf[t, WIN, j] = zero_tile
    row = lax.broadcasted_iota(jnp.int32, (tile, tile), 0)

    send_relay(0)
    if heads > 2:
        send_own(2)
    send_relay(1)
    for head in range(3, heads):
        send_own(head)

    def tile_step(head, t):
        start = jnp.clip(start_ref[t, here], 0, count - WIN)
        rel = jnp.clip(start - here + OWN, 0, OWN)
        q = q_buf[head, t]
        g = g_buf[t, :, lanes(head)]

        def place(i):
            return i // times, i % times

        def scores(i, top):
            s, j = place(i)
            block = dot_nt(k_cur[rel + s, j], q) * (SCALE * LOG2E)
            block = jnp.where(row < count_ref[j, start + s], block, -jnp.inf)
            s_buf[i] = block
            return jnp.maximum(top, fold(block, jnp.max))

        top = looped(9, chunks, scores, jnp.full((8, tile), -jnp.inf, F32))
        top = jnp.max(top, axis=0, keepdims=True)

        def exps(i, total):
            s, j = place(i)
            block = jnp.exp2(s_buf[i] - top)
            s_buf[i] = block
            dp_buf[i] = dot_nt(v_cur[rel + s, j], g)
            return total + fold(block, jnp.sum)

        total = looped(9, chunks, exps, jnp.zeros((8, tile), F32))
        inverse = 1.0 / jnp.sum(total, axis=0, keepdims=True)

        def attend(i, att):
            s, j = place(i)
            probs = s_buf[i] * inverse
            s_buf[i] = probs
            weights = probs.astype(BF16)
            w_buf[t, s, j] = weights
            return att + dot_nn(vt_cur[rel + s, j], weights)

        att = looped(9, chunks, attend, jnp.zeros((DH, tile), F32))
        rounded = att.astype(BF16).astype(F32)
        att_buf[head, t] = rounded.T.astype(BF16)
        delta = jnp.sum(g.astype(F32).T * rounded, axis=0, keepdims=True)

        def back(i, dq):
            s, j = place(i)
            dscores = (s_buf[i] * (dp_buf[i] - delta)).astype(BF16)
            ds_buf[t, s, j] = dscores
            return dq + dot_nn(kt_cur[rel + s, j], dscores)

        dq = looped(9, chunks, back, jnp.zeros((DH, tile), F32))
        dq_buf[head, t] = (dq * SCALE).T.astype(BF16)

    def key_side(head):
        rels = [jnp.clip(start_ref[t, here] - here + OWN, 0, OWN) for t in range(times)]

        def parts(slot, j):
            dk = jnp.zeros((tile, DH), F32)
            dv = jnp.zeros((tile, DH), F32)
            for t in range(times):
                s = slot - rels[t]
                s = jnp.where((s >= 0) & (s < WIN), s, WIN)
                dk = dk + dot_nn(ds_buf[t, s, j], q_buf[head, t])
                dv = dv + dot_nn(w_buf[t, s, j], g_buf[t, :, lanes(head)])
            return dk * SCALE, dv

        for slot in (0, SLOTS - 1, 1, SLOTS - 2, OWN):

            def one(j, carry, slot=slot):
                pair = parts(slot, j)
                for which in range(2):
                    if slot == 0:
                        far_out[head, 0, which, j] = pair[which].astype(BF16)
                    elif slot == SLOTS - 1:
                        far_out[head, 1, which, j] = pair[which].astype(BF16)
                    elif slot == OWN:
                        own_sum[head, which, j] = pair[which]
                    else:
                        near_sum[head, 0 if slot < OWN else 1, which, j] = pair[which]
                return carry

            lax.fori_loop(0, times, one, 0, unroll=True)
            if slot in (0, SLOTS - 1):
                side = 0 if slot == 0 else 1

                @pl.when(head > 0)
                def _():
                    far_copy(head, side).start()

    def send_near(head):
        for side in range(2):
            far_copy(head, side).wait_recv()
            for which in range(2):

                def one(j, carry, which=which, side=side):
                    near_out[head, side, which, j] = (
                        near_sum[head, side, which, j]
                        + far_in[head, side, which, j].astype(F32)
                    ).astype(BF16)
                    return carry

                lax.fori_loop(0, times, one, 0)
            near_copy(head, side).start()

    def finish(head):
        for side in range(2):
            near_copy(head, side).wait_recv()

        def one(j, carry):
            for which, out in enumerate((dk_buf, dv_buf)):
                out[head, j] = (
                    own_sum[head, which, j]
                    + near_in[head, 0, which, j].astype(F32)
                    + near_in[head, 1, which, j].astype(F32)
                ).astype(BF16)
            return carry

        lax.fori_loop(0, times, one, 0)
        out_copy(2, head).start()
        out_copy(3, head).start()

    def head_step(head, carry):
        load(2, head).wait()

        @pl.when(head == 0)
        def _():
            grad_here().wait()
            grad_chip().wait_recv()
            for other in range(2):
                grad_arrival(other).wait_recv()

        for side in range(2):
            relay_copy(head, side).wait_recv()

        def stage(i, inner):
            slot, j = i // times, i % times
            keys = kv[head, slot, 0, j]
            values = kv[head, slot, 1, j]
            k_cur[slot, j] = keys
            v_cur[slot, j] = values
            kt_cur[slot, j] = keys.T
            vt_cur[slot, j] = values.T
            return inner

        lax.fori_loop(0, SLOTS * times, stage, 0)

        def visit(t, inner):
            tile_step(head, t)
            return inner

        lax.fori_loop(0, times, visit, 0)
        out_copy(0, head).start()
        out_copy(1, head).start()
        key_side(head)

        @pl.when(head == 0)
        def _():
            for later in range(2, heads):
                send_relay(later)
            for side in range(2):
                far_copy(head, side).start()

        @pl.when(head > 0)
        def _():
            send_near(head - 1)

        @pl.when(head > 1)
        def _():
            finish(head - 2)

        return carry

    lax.fori_loop(0, heads, head_step, 0)
    send_near(heads - 1)
    finish(heads - 2)
    finish(heads - 1)

    def drain(head, carry):
        for side in range(2):
            own_copy(head, side).wait_send()
            relay_copy(head, side).wait_send()
            far_copy(head, side).wait_send()
            near_copy(head, side).wait_send()
        for which in range(4):
            out_copy(which, head).wait()
        return carry

    lax.fori_loop(0, heads, drain, 0)
    grad_chip().wait_send()
    for other in range(2):
        grad_arrival(other).wait_send()

    @pl.when(special)
    def _():
        for other in range(2):
            grad_half(other).wait_send()


def forward(times, *refs):
    sources, targets = refs[:4], refs[4:8]
    held, in_sem, out_sem = refs[8:]
    pieces = [(i, t) for t in range(times) for i in range(4)]
    inward = [
        pltpu.make_async_copy(sources[i].at[t], held.at[i, t], in_sem.at[i, t]) for i, t in pieces
    ]
    outward = [
        pltpu.make_async_copy(held.at[i, t], targets[i].at[t], out_sem.at[i, t]) for i, t in pieces
    ]
    for copy in inward:
        copy.start()
    for first, second in zip(inward, outward):
        first.wait()
        second.start()
    for copy in outward:
        copy.wait()


def shards(queries, keys, values, grad_out, window_start, key_counts):
    _, times, tile, width = queries.shape
    heads = width // DH
    groups = tile // grad_out.shape[2]
    block = (times, tile, DH)
    dma = pltpu.SemaphoreType.DMA
    any_spec = pl.BlockSpec(memory_space=pl.ANY)
    smem_spec = pl.BlockSpec(memory_space=pltpu.SMEM)
    out = jax.ShapeDtypeStruct((times, tile, width), BF16)
    pairs = times * heads * 6 * tile * WIN * times * tile * DH * 2
    results = pl.pallas_call(
        functools.partial(kernel, heads, times, tile, groups),
        out_shape=(out,) * 4,
        in_specs=[smem_spec, smem_spec] + [any_spec] * 4,
        out_specs=(any_spec,) * 4,
        scratch_shapes=[
            pltpu.VMEM((heads, SLOTS, 2) + block, BF16),
            pltpu.VMEM((heads, 2, 2) + block, BF16),
            pltpu.VMEM((heads, 2, 2) + block, BF16),
            pltpu.VMEM((heads, 2, 2) + block, BF16),
            pltpu.VMEM((heads, 2, 2) + block, BF16),
            pltpu.VMEM((heads, 2, 2) + block, F32),
            pltpu.VMEM((heads, 2) + block, F32),
            pltpu.VMEM((heads,) + block, BF16),
            pltpu.VMEM((times, tile, width), BF16),
            pltpu.VMEM((heads,) + block, BF16),
            pltpu.VMEM((heads,) + block, BF16),
            pltpu.VMEM((heads,) + block, BF16),
            pltpu.VMEM((heads,) + block, BF16),
            pltpu.VMEM((SLOTS, times, tile, DH), BF16),
            pltpu.VMEM((SLOTS, times, tile, DH), BF16),
            pltpu.VMEM((SLOTS, times, DH, tile), BF16),
            pltpu.VMEM((SLOTS, times, DH, tile), BF16),
            pltpu.VMEM((WIN * times, tile, tile), F32),
            pltpu.VMEM((WIN * times, tile, tile), F32),
            pltpu.VMEM((times, WIN + 1, times, tile, tile), BF16),
            pltpu.VMEM((times, WIN + 1, times, tile, tile), BF16),
            dma((heads, 3)),
            dma,
            dma,
            dma,
            dma((2,)),
            dma((2,)),
            dma((2,)),
            dma((2,)),
            pltpu.VMEM((2, times, tile // groups, width), BF16),
            dma((heads, 2)),
            dma((heads, 2)),
            dma((heads, 2)),
            dma((heads, 2)),
            dma((heads, 2)),
            dma((heads, 2)),
            dma((heads, 2)),
            dma((heads, 2)),
            dma((4, heads)),
        ],
        compiler_params=pltpu.CompilerParams(
            collective_id=0, has_side_effects=True, vmem_limit_bytes=60 * 1024 * 1024
        ),
        cost_estimate=pl.CostEstimate(
            flops=pairs, bytes_accessed=8 * times * tile * width * 2, transcendentals=0
        ),
        name="band_attention",
    )(window_start.T, key_counts.T, queries[0], keys[0], values[0], grad_out[0])
    results = pl.pallas_call(
        functools.partial(forward, times),
        out_shape=(out,) * 4,
        in_specs=[any_spec] * 4,
        out_specs=(any_spec,) * 4,
        scratch_shapes=[
            pltpu.VMEM((4, times, tile, width), BF16),
            dma((4, times)),
            dma((4, times)),
        ],
        name="place_results",
    )(*results)
    return tuple(result[None] for result in results)


def solution(mesh):
    placed = (
        P("ctx", None, None, "head"),
        P("ctx", None, None, "head"),
        P("ctx", None, None, "head"),
        P("ctx", None, "head", None),
        P(),
        P(),
    )
    return jax.shard_map(
        shards,
        mesh=mesh,
        in_specs=placed,
        out_specs=(P("ctx", None, None, "head"),) * 4,
        check_vma=False,
    )
```

```python
import functools

import jax
import jax.numpy as jnp
from jax import lax
from jax.experimental import pallas as pl
from jax.experimental.pallas import tpu as pltpu
from jax.sharding import PartitionSpec as P

DH = 128
WIN = 3
SLOTS = 2 * WIN - 1
OWN = WIN - 1
RUN = 8
SCALE = DH ** (-0.5)
LOG2E = 1.4426950408889634
MESH = pl.DeviceIdType.MESH
F32 = jnp.float32
BF16 = jnp.bfloat16

NT = (((1,), (1,)), ((), ()))


def dot_nt(a, b):
    return lax.dot_general(a, b, NT, preferred_element_type=F32)


def dot_nn(a, b):
    return jnp.dot(a, b, preferred_element_type=F32)


def looped(unroll, count, body, carry):
    return lax.fori_loop(0, count, body, carry, unroll=unroll)


def fold(block, op):
    rows, lanes = block.shape
    return op(block.reshape(rows // 8, 8, lanes), axis=0)


class Guarded:
    def __init__(self, copy, sends, receives):
        self.copy, self.sends, self.receives = copy, sends, receives

    def start(self):
        pl.when(self.sends)(lambda: self.copy.start())

    def wait_send(self):
        pl.when(self.sends)(lambda: self.copy.wait_send())

    def wait_recv(self):
        pl.when(self.receives)(lambda: self.copy.wait_recv())


def kernel(
    heads,
    times,
    tile,
    groups,
    start_ref,
    count_ref,
    q_hbm,
    k_hbm,
    v_hbm,
    g_hbm,
    att_ref,
    dq_ref,
    dk_ref,
    dv_ref,
    kv,
    far_out,
    far_in,
    near_out,
    near_in,
    near_sum,
    own_sum,
    q_buf,
    g_buf,
    k_cur,
    v_cur,
    kt_cur,
    vt_cur,
    s_buf,
    dp_buf,
    w_buf,
    ds_buf,
    load_sem,
    g_here,
    chip_send,
    chip_recv,
    cross_send,
    cross_recv,
    half_send,
    half_recv,
    g_mid,
    own_send,
    own_recv,
    relay_send,
    relay_recv,
    far_send,
    far_recv,
    near_send,
    near_recv,
):
    count = lax.axis_size("ctx")
    here = lax.axis_index("ctx")
    group = lax.axis_index("head")
    left = lax.rem(here + count - 1, count)
    right = lax.rem(here + 1, count)
    toward = (left, right)
    part = tile // groups
    chunks = WIN * times
    pair, core = group // 2, group % 2
    half = count // 2
    partner = lax.rem(here + half, count)
    flip = (here == half - RUN) | (here == half + RUN - 1)
    special = flip | (here == RUN - 1) | (here == count - RUN)
    next_pair = jnp.where(flip, 1 - pair, pair)
    width = heads * DH

    def lanes(head):
        return pl.ds(pl.multiple_of(head * DH, DH), DH)

    def load(which, head):
        source, target = (
            (k_hbm, kv.at[head, OWN, 0]),
            (v_hbm, kv.at[head, OWN, 1]),
            (q_hbm, q_buf.at[head]),
        )[which]
        return pltpu.make_async_copy(
            source.at[:, :, lanes(head)], target, load_sem.at[head, which]
        )

    def remote(source, target, sends, recvs, head, side):
        copy = pltpu.make_async_remote_copy(
            src_ref=source,
            dst_ref=target,
            send_sem=sends.at[head, side],
            recv_sem=recvs.at[head, side],
            device_id=(toward[side], group),
            device_id_type=MESH,
        )
        ends = (here > 0, here < count - 1)
        return Guarded(copy, ends[side], ends[1 - side])

    def own_copy(head, side):
        slot = OWN + 1 if side == 0 else OWN - 1
        return remote(kv.at[head, OWN], kv.at[head, slot], own_send, own_recv, head, side)

    def relay_copy(head, side):
        slot = OWN + 1 if side == 0 else OWN - 1
        target = OWN + 2 if side == 0 else OWN - 2
        return remote(kv.at[head, slot], kv.at[head, target], relay_send, relay_recv, head, side)

    def far_copy(head, side):
        return remote(
            far_out.at[head, side], far_in.at[head, side], far_send, far_recv, head, side
        )

    def near_copy(head, side, which):
        return remote(
            near_out.at[head, side, which],
            near_in.at[head, side, which],
            near_send.at[which],
            near_recv.at[which],
            head,
            side,
        )

    def grad_rows(owner):
        return g_buf.at[:, pl.ds(pl.multiple_of(owner * part, part), part), :]

    def grad_lanes(owner):
        return g_hbm.at[:, :, pl.ds(pl.multiple_of(owner * width, width), width)]

    def grad_chip():
        peer = pair * 2 + 1 - core
        return pltpu.make_async_remote_copy(
            src_ref=grad_lanes(peer),
            dst_ref=grad_rows(group),
            send_sem=chip_send,
            recv_sem=chip_recv,
            device_id=(here, peer),
            device_id_type=MESH,
        )

    def grad_cross(other):
        peer = (1 - pair) * 2 + other
        return pltpu.make_async_remote_copy(
            src_ref=grad_lanes(peer),
            dst_ref=grad_rows(group),
            send_sem=cross_send.at[other],
            recv_sem=cross_recv.at[core],
            device_id=(here, peer),
            device_id_type=MESH,
        )

    def grad_half(other):
        return pltpu.make_async_remote_copy(
            src_ref=grad_lanes((1 - pair) * 2 + other),
            dst_ref=g_mid.at[other],
            send_sem=half_send.at[other],
            recv_sem=half_recv.at[other],
            device_id=(partner, next_pair * 2 + core),
            device_id_type=MESH,
        )

    def grad_onward(other):
        return pltpu.make_async_remote_copy(
            src_ref=g_mid.at[other],
            dst_ref=grad_rows((1 - next_pair) * 2 + core),
            send_sem=cross_send.at[other],
            recv_sem=cross_recv.at[core],
            device_id=(partner, next_pair * 2 + other),
            device_id_type=MESH,
        )

    def grad_arrival(other):
        return pltpu.make_async_remote_copy(
            src_ref=g_mid.at[other],
            dst_ref=grad_rows((1 - pair) * 2 + other),
            send_sem=cross_send.at[other],
            recv_sem=cross_recv.at[other],
            device_id=(here, (1 - pair) * 2 + other),
            device_id_type=MESH,
        )

    def grad_here():
        return pltpu.make_async_copy(grad_lanes(group), grad_rows(group), g_here)

    for head in range(heads):
        for which in range(3):
            load(which, head).start()
    grad_here().start()

    barrier = pltpu.get_barrier_semaphore()
    for neighbour in toward:
        pl.semaphore_signal(barrier, inc=1, device_id=(neighbour, group), device_id_type=MESH)
    for step in range(1, groups):
        pl.semaphore_signal(
            barrier,
            inc=1,
            device_id=(here, lax.rem(group + step, groups)),
            device_id_type=MESH,
        )

    @pl.when(special)
    def _():
        for peer in range(groups):
            pl.semaphore_signal(barrier, inc=1, device_id=(partner, peer), device_id_type=MESH)

    pl.semaphore_wait(barrier, 2 + groups - 1 + jnp.where(special, groups, 0))

    zero_block = jnp.zeros(kv.shape[2:], BF16)
    for empty, side, slots in ((here == 0, 1, (0, 1)), (here == count - 1, 0, (3, 4))):

        @pl.when(empty)
        def _():
            def clear(head, carry):
                for slot in slots:
                    kv[head, slot] = zero_block
                far_in[head, side] = zero_block
                near_in[head, side] = zero_block
                return carry

            lax.fori_loop(0, heads, clear, 0)

    def send_own(head):
        load(0, head).wait()
        load(1, head).wait()
        for side in range(2):
            own_copy(head, side).start()

    def send_relay(head):
        for side in (1, 0):
            own_copy(head, side).wait_recv()
            relay_copy(head, side).start()

    send_own(0)
    grad_chip().start()

    @pl.when(special)
    def _():
        for other in range(2):
            grad_half(other).start()

    @pl.when(jnp.logical_not(special))
    def _():
        for other in range(2):
            grad_cross(other).start()

    send_own(1)

    @pl.when(special)
    def _():
        for other in range(2):
            grad_half(other).wait_recv()
            grad_onward(other).start()


    zero_tile = jnp.zeros((tile, tile), BF16)
    for t in range(times):
        for j in range(times):
            w_buf[t, WIN, j] = zero_tile
            ds_buf[t, WIN, j] = zero_tile
    row = lax.broadcasted_iota(jnp.int32, (tile, tile), 0)

    send_relay(0)
    if heads > 2:
        send_own(2)
    send_relay(1)
    for head in range(3, heads):
        send_own(head)

    def tile_step(head, t):
        start = jnp.clip(start_ref[t, here], 0, count - WIN)
        rel = jnp.clip(start - here + OWN, 0, OWN)
        q = q_buf[head, t]
        g = g_buf[t, :, lanes(head)]

        def place(i):
            return i // times, i % times

        def scores(i, top):
            s, j = place(i)
            block = dot_nt(k_cur[rel + s, j], q) * (SCALE * LOG2E)
            block = jnp.where(row < count_ref[j, start + s], block, -jnp.inf)
            s_buf[i] = block
            return jnp.maximum(top, fold(block, jnp.max))

        top = looped(9, chunks, scores, jnp.full((8, tile), -jnp.inf, F32))
        top = jnp.max(top, axis=0, keepdims=True)

        def exps(i, total):
            s, j = place(i)
            block = jnp.exp2(s_buf[i] - top)
            s_buf[i] = block
            dp_buf[i] = dot_nt(v_cur[rel + s, j], g)
            return total + fold(block, jnp.sum)

        total = looped(9, chunks, exps, jnp.zeros((8, tile), F32))
        inverse = 1.0 / jnp.sum(total, axis=0, keepdims=True)

        def attend(i, att):
            s, j = place(i)
            probs = s_buf[i] * inverse
            s_buf[i] = probs
            weights = probs.astype(BF16)
            w_buf[t, s, j] = weights
            return att + dot_nn(vt_cur[rel + s, j], weights)

        att = looped(9, chunks, attend, jnp.zeros((DH, tile), F32))
        rounded = att.astype(BF16).astype(F32)
        att_ref[t, :, lanes(head)] = rounded.T.astype(BF16)
        delta = jnp.sum(g.astype(F32).T * rounded, axis=0, keepdims=True)

        def back(i, dq):
            s, j = place(i)
            dscores = (s_buf[i] * (dp_buf[i] - delta)).astype(BF16)
            ds_buf[t, s, j] = dscores
            return dq + dot_nn(kt_cur[rel + s, j], dscores)

        dq = looped(9, chunks, back, jnp.zeros((DH, tile), F32))
        dq_ref[t, :, lanes(head)] = (dq * SCALE).T.astype(BF16)

    def key_side(head):
        rels = [jnp.clip(start_ref[t, here] - here + OWN, 0, OWN) for t in range(times)]

        def parts(slot, j):
            dk = jnp.zeros((tile, DH), F32)
            dv = jnp.zeros((tile, DH), F32)
            for t in range(times):
                s = slot - rels[t]
                s = jnp.where((s >= 0) & (s < WIN), s, WIN)
                dk = dk + dot_nn(ds_buf[t, s, j], q_buf[head, t])
                dv = dv + dot_nn(w_buf[t, s, j], g_buf[t, :, lanes(head)])
            return dk * SCALE, dv

        for slot in (0, SLOTS - 1, 1, SLOTS - 2, OWN):

            def one(j, carry, slot=slot):
                pair = parts(slot, j)
                for which in range(2):
                    if slot == 0:
                        far_out[head, 0, which, j] = pair[which].astype(BF16)
                    elif slot == SLOTS - 1:
                        far_out[head, 1, which, j] = pair[which].astype(BF16)
                    elif slot == OWN:
                        own_sum[head, which, j] = pair[which]
                    else:
                        near_sum[head, 0 if slot < OWN else 1, which, j] = pair[which]
                return carry

            lax.fori_loop(0, times, one, 0, unroll=True)
            if slot in (0, SLOTS - 1):
                side = 0 if slot == 0 else 1

                @pl.when(head > 0)
                def _():
                    far_copy(head, side).start()

    def send_near(head):
        for side in range(2):
            far_copy(head, side).wait_recv()
            for which in range(2):

                def one(j, carry, which=which, side=side):
                    near_out[head, side, which, j] = (
                        near_sum[head, side, which, j]
                        + far_in[head, side, which, j].astype(F32)
                    ).astype(BF16)
                    return carry

                lax.fori_loop(0, times, one, 0)
                near_copy(head, side, which).start()

    def finish(head):
        for which, out in enumerate((dk_ref, dv_ref)):
            for side in range(2):
                near_copy(head, side, which).wait_recv()

            def one(j, carry, which=which, out=out):
                out[j, :, lanes(head)] = (
                    own_sum[head, which, j]
                    + near_in[head, 0, which, j].astype(F32)
                    + near_in[head, 1, which, j].astype(F32)
                ).astype(BF16)
                return carry

            lax.fori_loop(0, times, one, 0)

    def head_step(head, carry):
        load(2, head).wait()

        @pl.when(head == 0)
        def _():
            grad_here().wait()
            grad_chip().wait_recv()
            for other in range(2):
                grad_arrival(other).wait_recv()

        for side in range(2):
            relay_copy(head, side).wait_recv()

        def stage(i, inner):
            slot, j = i // times, i % times
            keys = kv[head, slot, 0, j]
            values = kv[head, slot, 1, j]
            k_cur[slot, j] = keys
            v_cur[slot, j] = values
            kt_cur[slot, j] = keys.T
            vt_cur[slot, j] = values.T
            return inner

        lax.fori_loop(0, SLOTS * times, stage, 0)

        def visit(t, inner):
            tile_step(head, t)

            @pl.when((head == 0) & (t == 1))
            def _():
                send_relay(2)

            @pl.when((head == 1) & (t == 1))
            def _():
                send_relay(3)
                for side in range(2):
                    far_copy(0, side).start()

            return inner

        lax.fori_loop(0, times, visit, 0)
        key_side(head)

        @pl.when(head > 1)
        def _():
            send_near(head - 2)

        return carry

    lax.fori_loop(0, heads, head_step, 0)
    for head in range(heads - 2, heads):
        send_near(head)
    for head in range(heads):
        finish(head)

    def drain(head, carry):
        for side in range(2):
            own_copy(head, side).wait_send()
            relay_copy(head, side).wait_send()
            far_copy(head, side).wait_send()
            for which in range(2):
                near_copy(head, side, which).wait_send()
        return carry

    lax.fori_loop(0, heads, drain, 0)
    grad_chip().wait_send()
    for other in range(2):
        grad_arrival(other).wait_send()

    @pl.when(special)
    def _():
        for other in range(2):
            grad_half(other).wait_send()


def forward(times, *refs):
    sources, targets, sems = refs[:4], refs[4:8], refs[8]
    copies = [
        pltpu.make_async_copy(sources[i].at[t], targets[i].at[t], sems.at[i, t])
        for t in range(times)
        for i in range(4)
    ]
    for copy in copies:
        copy.start()
    for copy in copies:
        copy.wait()


def shards(queries, keys, values, grad_out, window_start, key_counts):
    _, times, tile, width = queries.shape
    heads = width // DH
    groups = tile // grad_out.shape[2]
    block = (times, tile, DH)
    dma = pltpu.SemaphoreType.DMA
    any_spec = pl.BlockSpec(memory_space=pl.ANY)
    vmem_spec = pl.BlockSpec(memory_space=pltpu.VMEM)
    smem_spec = pl.BlockSpec(memory_space=pltpu.SMEM)
    out = jax.ShapeDtypeStruct((times, tile, width), BF16)
    pairs = times * heads * 6 * tile * WIN * times * tile * DH * 2
    results = pl.pallas_call(
        functools.partial(kernel, heads, times, tile, groups),
        out_shape=(pltpu.VMEM(out.shape, BF16),) * 4,
        in_specs=[smem_spec, smem_spec] + [any_spec] * 4,
        out_specs=(vmem_spec,) * 4,
        scratch_shapes=[
            pltpu.VMEM((heads, SLOTS, 2) + block, BF16),
            pltpu.VMEM((heads, 2, 2) + block, BF16),
            pltpu.VMEM((heads, 2, 2) + block, BF16),
            pltpu.VMEM((heads, 2, 2) + block, BF16),
            pltpu.VMEM((heads, 2, 2) + block, BF16),
            pltpu.VMEM((heads, 2, 2) + block, F32),
            pltpu.VMEM((heads, 2) + block, F32),
            pltpu.VMEM((heads,) + block, BF16),
            pltpu.VMEM((times, tile, width), BF16),
            pltpu.VMEM((SLOTS, times, tile, DH), BF16),
            pltpu.VMEM((SLOTS, times, tile, DH), BF16),
            pltpu.VMEM((SLOTS, times, DH, tile), BF16),
            pltpu.VMEM((SLOTS, times, DH, tile), BF16),
            pltpu.VMEM((WIN * times, tile, tile), F32),
            pltpu.VMEM((WIN * times, tile, tile), F32),
            pltpu.VMEM((times, WIN + 1, times, tile, tile), BF16),
            pltpu.VMEM((times, WIN + 1, times, tile, tile), BF16),
            dma((heads, 3)),
            dma,
            dma,
            dma,
            dma((2,)),
            dma((2,)),
            dma((2,)),
            dma((2,)),
            pltpu.VMEM((2, times, tile // groups, width), BF16),
            dma((heads, 2)),
            dma((heads, 2)),
            dma((heads, 2)),
            dma((heads, 2)),
            dma((heads, 2)),
            dma((heads, 2)),
            dma((2, heads, 2)),
            dma((2, heads, 2)),
        ],
        compiler_params=pltpu.CompilerParams(
            collective_id=0, has_side_effects=True, vmem_limit_bytes=54 * 1024 * 1024
        ),
        cost_estimate=pl.CostEstimate(
            flops=pairs, bytes_accessed=8 * times * tile * width * 2, transcendentals=0
        ),
        name="band_attention",
    )(window_start.T, key_counts.T, queries[0], keys[0], values[0], grad_out[0])
    results = pl.pallas_call(
        functools.partial(forward, times),
        out_shape=(out,) * 4,
        in_specs=[vmem_spec] * 4,
        out_specs=(any_spec,) * 4,
        scratch_shapes=[dma((4, times))],
        compiler_params=pltpu.CompilerParams(vmem_limit_bytes=4 * 1024 * 1024),
        name="place_results",
    )(*results)
    return tuple(result[None] for result in results)


def solution(mesh):
    placed = (
        P("ctx", None, None, "head"),
        P("ctx", None, None, "head"),
        P("ctx", None, None, "head"),
        P("ctx", None, "head", None),
        P(),
        P(),
    )
    return jax.shard_map(
        shards,
        mesh=mesh,
        in_specs=placed,
        out_specs=(P("ctx", None, None, "head"),) * 4,
        check_vma=False,
    )
```

```python
import functools

import jax
import jax.numpy as jnp
from jax import lax
from jax.experimental import pallas as pl
from jax.experimental.pallas import tpu as pltpu
from jax.sharding import PartitionSpec as P

DH = 128
WIN = 3
SLOTS = 2 * WIN - 1
OWN = WIN - 1
RUN = 8
SCALE = DH ** (-0.5)
LOG2E = 1.4426950408889634
MESH = pl.DeviceIdType.MESH
F32 = jnp.float32
BF16 = jnp.bfloat16

NT = (((1,), (1,)), ((), ()))


def dot_nt(a, b):
    return lax.dot_general(a, b, NT, preferred_element_type=F32)


def dot_nn(a, b):
    return jnp.dot(a, b, preferred_element_type=F32)


def looped(unroll, count, body, carry):
    return lax.fori_loop(0, count, body, carry, unroll=unroll)


def fold(block, op):
    rows, lanes = block.shape
    return op(block.reshape(rows // 8, 8, lanes), axis=0)


class Guarded:
    def __init__(self, copy, sends, receives):
        self.copy, self.sends, self.receives = copy, sends, receives

    def start(self):
        pl.when(self.sends)(lambda: self.copy.start())

    def wait_send(self):
        pl.when(self.sends)(lambda: self.copy.wait_send())

    def wait_recv(self):
        pl.when(self.receives)(lambda: self.copy.wait_recv())


def kernel(
    heads,
    times,
    tile,
    groups,
    start_ref,
    count_ref,
    q_hbm,
    k_hbm,
    v_hbm,
    g_hbm,
    att_ref,
    dq_ref,
    dk_ref,
    dv_ref,
    kv,
    far_out,
    far_in,
    near_out,
    near_in,
    near_sum,
    own_sum,
    q_buf,
    g_buf,
    k_cur,
    v_cur,
    kt_cur,
    vt_cur,
    s_buf,
    dp_buf,
    w_buf,
    ds_buf,
    load_sem,
    g_here,
    chip_send,
    chip_recv,
    cross_send,
    cross_recv,
    half_send,
    half_recv,
    g_mid,
    own_send,
    own_recv,
    relay_send,
    relay_recv,
    far_send,
    far_recv,
    near_send,
    near_recv,
):
    count = lax.axis_size("ctx")
    here = lax.axis_index("ctx")
    group = lax.axis_index("head")
    left = lax.rem(here + count - 1, count)
    right = lax.rem(here + 1, count)
    toward = (left, right)
    part = tile // groups
    chunks = WIN * times
    pair, core = group // 2, group % 2
    half = count // 2
    partner = lax.rem(here + half, count)
    flip = (here == half - RUN) | (here == half + RUN - 1)
    special = flip | (here == RUN - 1) | (here == count - RUN)
    next_pair = jnp.where(flip, 1 - pair, pair)
    width = heads * DH

    def lanes(head):
        return pl.ds(pl.multiple_of(head * DH, DH), DH)

    def load(which, head):
        source, target = (
            (k_hbm, kv.at[head, OWN, 0]),
            (v_hbm, kv.at[head, OWN, 1]),
            (q_hbm, q_buf.at[head]),
        )[which]
        return pltpu.make_async_copy(
            source.at[:, :, lanes(head)], target, load_sem.at[head, which]
        )

    def remote(source, target, sends, recvs, head, side):
        copy = pltpu.make_async_remote_copy(
            src_ref=source,
            dst_ref=target,
            send_sem=sends.at[head, side],
            recv_sem=recvs.at[head, side],
            device_id=(toward[side], group),
            device_id_type=MESH,
        )
        ends = (here > 0, here < count - 1)
        return Guarded(copy, ends[side], ends[1 - side])

    def own_copy(head, side):
        slot = OWN + 1 if side == 0 else OWN - 1
        return remote(kv.at[head, OWN], kv.at[head, slot], own_send, own_recv, head, side)

    def relay_copy(head, side):
        slot = OWN + 1 if side == 0 else OWN - 1
        target = OWN + 2 if side == 0 else OWN - 2
        return remote(kv.at[head, slot], kv.at[head, target], relay_send, relay_recv, head, side)

    def far_copy(head, side):
        return remote(
            far_out.at[head, side], far_in.at[head, side], far_send, far_recv, head, side
        )

    def near_copy(head, side, which):
        return remote(
            near_out.at[head, side, which],
            near_in.at[head, side, which],
            near_send.at[which],
            near_recv.at[which],
            head,
            side,
        )

    def grad_rows(owner):
        return g_buf.at[:, pl.ds(pl.multiple_of(owner * part, part), part), :]

    def grad_lanes(owner):
        return g_hbm.at[:, :, pl.ds(pl.multiple_of(owner * width, width), width)]

    def grad_chip():
        peer = pair * 2 + 1 - core
        return pltpu.make_async_remote_copy(
            src_ref=grad_lanes(peer),
            dst_ref=grad_rows(group),
            send_sem=chip_send,
            recv_sem=chip_recv,
            device_id=(here, peer),
            device_id_type=MESH,
        )

    def grad_cross(other):
        peer = (1 - pair) * 2 + other
        return pltpu.make_async_remote_copy(
            src_ref=grad_lanes(peer),
            dst_ref=grad_rows(group),
            send_sem=cross_send.at[other],
            recv_sem=cross_recv.at[core],
            device_id=(here, peer),
            device_id_type=MESH,
        )

    def grad_half(other):
        return pltpu.make_async_remote_copy(
            src_ref=grad_lanes((1 - pair) * 2 + other),
            dst_ref=g_mid.at[other],
            send_sem=half_send.at[other],
            recv_sem=half_recv.at[other],
            device_id=(partner, next_pair * 2 + core),
            device_id_type=MESH,
        )

    def grad_onward(other):
        return pltpu.make_async_remote_copy(
            src_ref=g_mid.at[other],
            dst_ref=grad_rows((1 - next_pair) * 2 + core),
            send_sem=cross_send.at[other],
            recv_sem=cross_recv.at[core],
            device_id=(partner, next_pair * 2 + other),
            device_id_type=MESH,
        )

    def grad_arrival(other):
        return pltpu.make_async_remote_copy(
            src_ref=g_mid.at[other],
            dst_ref=grad_rows((1 - pair) * 2 + other),
            send_sem=cross_send.at[other],
            recv_sem=cross_recv.at[other],
            device_id=(here, (1 - pair) * 2 + other),
            device_id_type=MESH,
        )

    def grad_here():
        return pltpu.make_async_copy(grad_lanes(group), grad_rows(group), g_here)


    barrier = pltpu.get_barrier_semaphore()
    for neighbour in toward:
        pl.semaphore_signal(barrier, inc=1, device_id=(neighbour, group), device_id_type=MESH)
    for step in range(1, groups):
        pl.semaphore_signal(
            barrier,
            inc=1,
            device_id=(here, lax.rem(group + step, groups)),
            device_id_type=MESH,
        )

    @pl.when(special)
    def _():
        for peer in range(groups):
            pl.semaphore_signal(barrier, inc=1, device_id=(partner, peer), device_id_type=MESH)

    for which in range(2):
        load(which, 0).start()
    pl.semaphore_wait(barrier, 2 + groups - 1 + jnp.where(special, groups, 0))

    def send_own(head):
        load(0, head).wait()
        load(1, head).wait()
        for side in range(2):
            own_copy(head, side).start()

    def send_relay(head):
        for side in (1, 0):
            own_copy(head, side).wait_recv()
            relay_copy(head, side).start()

    send_own(0)
    for which in range(2):
        load(which, 1).start()
    grad_chip().start()

    @pl.when(special)
    def _():
        for other in range(2):
            grad_half(other).start()

    @pl.when(jnp.logical_not(special))
    def _():
        for other in range(2):
            grad_cross(other).start()

    send_own(1)
    for head in range(heads):
        for which in range(3):
            if which == 2 or head > 1:
                load(which, head).start()
    grad_here().start()

    zero_block = jnp.zeros(kv.shape[2:], BF16)
    for empty, side, slots in ((here == 0, 1, (0, 1)), (here == count - 1, 0, (3, 4))):

        @pl.when(empty)
        def _():
            def clear(head, carry):
                for slot in slots:
                    kv[head, slot] = zero_block
                far_in[head, side] = zero_block
                near_in[head, side] = zero_block
                return carry

            lax.fori_loop(0, heads, clear, 0)

    @pl.when(special)
    def _():
        for other in range(2):
            grad_half(other).wait_recv()
            grad_onward(other).start()

    zero_tile = jnp.zeros((tile, tile), BF16)
    for t in range(times):
        for j in range(times):
            w_buf[t, WIN, j] = zero_tile
            ds_buf[t, WIN, j] = zero_tile
    row = lax.broadcasted_iota(jnp.int32, (tile, tile), 0)

    send_relay(0)
    if heads > 2:
        send_own(2)
    send_relay(1)
    for head in range(3, heads):
        send_own(head)

    def tile_step(head, t):
        start = jnp.clip(start_ref[t, here], 0, count - WIN)
        rel = jnp.clip(start - here + OWN, 0, OWN)
        q = q_buf[head, t]
        g = g_buf[t, :, lanes(head)]

        def place(i):
            return i // times, i % times

        def scores(i, top):
            s, j = place(i)
            block = dot_nt(k_cur[rel + s, j], q) * (SCALE * LOG2E)
            block = jnp.where(row < count_ref[j, start + s], block, -jnp.inf)
            s_buf[i] = block
            return jnp.maximum(top, fold(block, jnp.max))

        top = looped(9, chunks, scores, jnp.full((8, tile), -jnp.inf, F32))
        top = jnp.max(top, axis=0, keepdims=True)

        def exps(i, total):
            s, j = place(i)
            block = jnp.exp2(s_buf[i] - top)
            s_buf[i] = block
            dp_buf[i] = dot_nt(v_cur[rel + s, j], g)
            return total + fold(block, jnp.sum)

        total = looped(9, chunks, exps, jnp.zeros((8, tile), F32))
        inverse = 1.0 / jnp.sum(total, axis=0, keepdims=True)

        def attend(i, att):
            s, j = place(i)
            probs = s_buf[i] * inverse
            s_buf[i] = probs
            weights = probs.astype(BF16)
            w_buf[t, s, j] = weights
            return att + dot_nn(vt_cur[rel + s, j], weights)

        att = looped(9, chunks, attend, jnp.zeros((DH, tile), F32))
        rounded = att.astype(BF16).astype(F32)
        att_ref[t, :, lanes(head)] = rounded.T.astype(BF16)
        delta = jnp.sum(g.astype(F32).T * rounded, axis=0, keepdims=True)

        def back(i, dq):
            s, j = place(i)
            dscores = (s_buf[i] * (dp_buf[i] - delta)).astype(BF16)
            ds_buf[t, s, j] = dscores
            return dq + dot_nn(kt_cur[rel + s, j], dscores)

        dq = looped(9, chunks, back, jnp.zeros((DH, tile), F32))
        dq_ref[t, :, lanes(head)] = (dq * SCALE).T.astype(BF16)

    def key_side(head):
        rels = [jnp.clip(start_ref[t, here] - here + OWN, 0, OWN) for t in range(times)]

        def parts(slot, j):
            dk = jnp.zeros((tile, DH), F32)
            dv = jnp.zeros((tile, DH), F32)
            for t in range(times):
                s = slot - rels[t]
                s = jnp.where((s >= 0) & (s < WIN), s, WIN)
                dk = dk + dot_nn(ds_buf[t, s, j], q_buf[head, t])
                dv = dv + dot_nn(w_buf[t, s, j], g_buf[t, :, lanes(head)])
            return dk * SCALE, dv

        for slot in (0, SLOTS - 1, 1, SLOTS - 2, OWN):

            def one(j, carry, slot=slot):
                pair = parts(slot, j)
                for which in range(2):
                    if slot == 0:
                        far_out[head, 0, which, j] = pair[which].astype(BF16)
                    elif slot == SLOTS - 1:
                        far_out[head, 1, which, j] = pair[which].astype(BF16)
                    elif slot == OWN:
                        own_sum[head, which, j] = pair[which]
                    else:
                        near_sum[head, 0 if slot < OWN else 1, which, j] = pair[which]
                return carry

            lax.fori_loop(0, times, one, 0, unroll=True)
            if slot in (0, SLOTS - 1):
                side = 0 if slot == 0 else 1

                @pl.when(head > 0)
                def _():
                    far_copy(head, side).start()

    def send_near(head):
        for side in range(2):
            far_copy(head, side).wait_recv()
            for which in range(2):

                def one(j, carry, which=which, side=side):
                    near_out[head, side, which, j] = (
                        near_sum[head, side, which, j]
                        + far_in[head, side, which, j].astype(F32)
                    ).astype(BF16)
                    return carry

                lax.fori_loop(0, times, one, 0)
                near_copy(head, side, which).start()

    def finish(head):
        for which, out in enumerate((dk_ref, dv_ref)):
            for side in range(2):
                near_copy(head, side, which).wait_recv()

            def one(j, carry, which=which, out=out):
                out[j, :, lanes(head)] = (
                    own_sum[head, which, j]
                    + near_in[head, 0, which, j].astype(F32)
                    + near_in[head, 1, which, j].astype(F32)
                ).astype(BF16)
                return carry

            lax.fori_loop(0, times, one, 0)

    def head_step(head, carry):
        load(2, head).wait()

        @pl.when(head == 0)
        def _():
            grad_here().wait()
            grad_chip().wait_recv()
            for other in range(2):
                grad_arrival(other).wait_recv()

        for side in range(2):
            relay_copy(head, side).wait_recv()

        def stage(i, inner):
            slot, j = i // times, i % times
            keys = kv[head, slot, 0, j]
            values = kv[head, slot, 1, j]
            k_cur[slot, j] = keys
            v_cur[slot, j] = values
            kt_cur[slot, j] = keys.T
            vt_cur[slot, j] = values.T
            return inner

        lax.fori_loop(0, SLOTS * times, stage, 0)

        def visit(t, inner):
            tile_step(head, t)

            @pl.when((head == 0) & (t == 1))
            def _():
                send_relay(2)

            @pl.when((head == 1) & (t == 1))
            def _():
                send_relay(3)
                for side in range(2):
                    far_copy(0, side).start()

            return inner

        lax.fori_loop(0, times, visit, 0)
        key_side(head)

        @pl.when(head > 1)
        def _():
            send_near(head - 2)

        return carry

    lax.fori_loop(0, heads, head_step, 0)
    for head in range(heads - 2, heads):
        send_near(head)
    for head in range(heads - 1):
        finish(head)

    def drain(head, carry):
        for side in range(2):
            own_copy(head, side).wait_send()
            relay_copy(head, side).wait_send()
            far_copy(head, side).wait_send()
        return carry

    def drain_near(head, carry):
        for side in range(2):
            for which in range(2):
                near_copy(head, side, which).wait_send()
        return carry

    lax.fori_loop(0, heads, drain, 0)
    lax.fori_loop(0, heads - 1, drain_near, 0)
    grad_chip().wait_send()
    for other in range(2):
        grad_arrival(other).wait_send()

    @pl.when(special)
    def _():
        for other in range(2):
            grad_half(other).wait_send()

    finish(heads - 1)
    drain_near(heads - 1, 0)


def forward(times, *refs):
    sources, targets, sems = refs[:4], refs[4:8], refs[8]
    copies = [
        pltpu.make_async_copy(sources[i].at[t], targets[i].at[t], sems.at[i, t])
        for t in range(times)
        for i in range(4)
    ]
    for copy in copies:
        copy.start()
    for copy in copies:
        copy.wait()


def shards(queries, keys, values, grad_out, window_start, key_counts):
    _, times, tile, width = queries.shape
    heads = width // DH
    groups = tile // grad_out.shape[2]
    block = (times, tile, DH)
    dma = pltpu.SemaphoreType.DMA
    any_spec = pl.BlockSpec(memory_space=pl.ANY)
    vmem_spec = pl.BlockSpec(memory_space=pltpu.VMEM)
    smem_spec = pl.BlockSpec(memory_space=pltpu.SMEM)
    out = jax.ShapeDtypeStruct((times, tile, width), BF16)
    pairs = times * heads * 6 * tile * WIN * times * tile * DH * 2
    results = pl.pallas_call(
        functools.partial(kernel, heads, times, tile, groups),
        out_shape=(pltpu.VMEM(out.shape, BF16),) * 4,
        in_specs=[smem_spec, smem_spec] + [any_spec] * 4,
        out_specs=(vmem_spec,) * 4,
        scratch_shapes=[
            pltpu.VMEM((heads, SLOTS, 2) + block, BF16),
            pltpu.VMEM((heads, 2, 2) + block, BF16),
            pltpu.VMEM((heads, 2, 2) + block, BF16),
            pltpu.VMEM((heads, 2, 2) + block, BF16),
            pltpu.VMEM((heads, 2, 2) + block, BF16),
            pltpu.VMEM((heads, 2, 2) + block, F32),
            pltpu.VMEM((heads, 2) + block, F32),
            pltpu.VMEM((heads,) + block, BF16),
            pltpu.VMEM((times, tile, width), BF16),
            pltpu.VMEM((SLOTS, times, tile, DH), BF16),
            pltpu.VMEM((SLOTS, times, tile, DH), BF16),
            pltpu.VMEM((SLOTS, times, DH, tile), BF16),
            pltpu.VMEM((SLOTS, times, DH, tile), BF16),
            pltpu.VMEM((WIN * times, tile, tile), F32),
            pltpu.VMEM((WIN * times, tile, tile), F32),
            pltpu.VMEM((times, WIN + 1, times, tile, tile), BF16),
            pltpu.VMEM((times, WIN + 1, times, tile, tile), BF16),
            dma((heads, 3)),
            dma,
            dma,
            dma,
            dma((2,)),
            dma((2,)),
            dma((2,)),
            dma((2,)),
            pltpu.VMEM((2, times, tile // groups, width), BF16),
            dma((heads, 2)),
            dma((heads, 2)),
            dma((heads, 2)),
            dma((heads, 2)),
            dma((heads, 2)),
            dma((heads, 2)),
            dma((2, heads, 2)),
            dma((2, heads, 2)),
        ],
        compiler_params=pltpu.CompilerParams(
            collective_id=0, has_side_effects=True, vmem_limit_bytes=54 * 1024 * 1024
        ),
        cost_estimate=pl.CostEstimate(
            flops=pairs, bytes_accessed=8 * times * tile * width * 2, transcendentals=0
        ),
        name="band_attention",
    )(window_start.T, key_counts.T, queries[0], keys[0], values[0], grad_out[0])
    results = pl.pallas_call(
        functools.partial(forward, times),
        out_shape=(out,) * 4,
        in_specs=[vmem_spec] * 4,
        out_specs=(any_spec,) * 4,
        scratch_shapes=[dma((4, times))],
        compiler_params=pltpu.CompilerParams(vmem_limit_bytes=4 * 1024 * 1024),
        name="place_results",
    )(*results)
    return tuple(result[None] for result in results)


def solution(mesh):
    placed = (
        P("ctx", None, None, "head"),
        P("ctx", None, None, "head"),
        P("ctx", None, None, "head"),
        P("ctx", None, "head", None),
        P(),
        P(),
    )
    return jax.shard_map(
        shards,
        mesh=mesh,
        in_specs=placed,
        out_specs=(P("ctx", None, None, "head"),) * 4,
        check_vma=False,
    )
```

```python
import functools

import jax
import jax.numpy as jnp
from jax import lax
from jax.experimental import pallas as pl
from jax.experimental.pallas import tpu as pltpu
from jax.sharding import PartitionSpec as P

DH = 128
WIN = 3
SLOTS = 2 * WIN - 1
OWN = WIN - 1
RUN = 8
SCALE = DH ** (-0.5)
LOG2E = 1.4426950408889634
MESH = pl.DeviceIdType.MESH
F32 = jnp.float32
BF16 = jnp.bfloat16

NT = (((1,), (1,)), ((), ()))


def dot_nt(a, b):
    return lax.dot_general(a, b, NT, preferred_element_type=F32)


def dot_nn(a, b):
    return jnp.dot(a, b, preferred_element_type=F32)


def looped(unroll, count, body, carry):
    return lax.fori_loop(0, count, body, carry, unroll=unroll)


def fold(block, op):
    rows, lanes = block.shape
    return op(block.reshape(rows // 8, 8, lanes), axis=0)


class Guarded:
    def __init__(self, copy, sends, receives):
        self.copy, self.sends, self.receives = copy, sends, receives

    def start(self):
        pl.when(self.sends)(lambda: self.copy.start())

    def wait_send(self):
        pl.when(self.sends)(lambda: self.copy.wait_send())

    def wait_recv(self):
        pl.when(self.receives)(lambda: self.copy.wait_recv())


def kernel(
    heads,
    times,
    tile,
    groups,
    start_ref,
    count_ref,
    q_hbm,
    k_hbm,
    v_hbm,
    g_hbm,
    att_ref,
    dq_ref,
    dk_ref,
    dv_ref,
    kv,
    far_out,
    far_in,
    near_out,
    near_in,
    near_sum,
    own_sum,
    q_buf,
    g_buf,
    k_cur,
    v_cur,
    kt_cur,
    vt_cur,
    s_buf,
    dp_buf,
    w_buf,
    ds_buf,
    load_sem,
    g_here,
    chip_send,
    chip_recv,
    cross_send,
    cross_recv,
    half_send,
    half_recv,
    g_mid,
    own_send,
    own_recv,
    relay_send,
    relay_recv,
    far_send,
    far_recv,
    near_send,
    near_recv,
):
    count = lax.axis_size("ctx")
    here = lax.axis_index("ctx")
    group = lax.axis_index("head")
    left = lax.rem(here + count - 1, count)
    right = lax.rem(here + 1, count)
    toward = (left, right)
    part = tile // groups
    chunks = WIN * times
    pair, core = group // 2, group % 2
    half = count // 2
    partner = lax.rem(here + half, count)
    flip = (here == half - RUN) | (here == half + RUN - 1)
    special = flip | (here == RUN - 1) | (here == count - RUN)
    next_pair = jnp.where(flip, 1 - pair, pair)
    width = heads * DH

    def lanes(head):
        return pl.ds(pl.multiple_of(head * DH, DH), DH)

    def load(which, head):
        source, target = (
            (k_hbm, kv.at[head, OWN, 0]),
            (v_hbm, kv.at[head, OWN, 1]),
            (q_hbm, q_buf.at[head]),
        )[which]
        return pltpu.make_async_copy(
            source.at[:, :, lanes(head)], target, load_sem.at[head, which]
        )

    def remote(source, target, sends, recvs, head, side):
        copy = pltpu.make_async_remote_copy(
            src_ref=source,
            dst_ref=target,
            send_sem=sends.at[head, side],
            recv_sem=recvs.at[head, side],
            device_id=(toward[side], group),
            device_id_type=MESH,
        )
        ends = (here > 0, here < count - 1)
        return Guarded(copy, ends[side], ends[1 - side])

    def own_copy(head, side):
        slot = OWN + 1 if side == 0 else OWN - 1
        return remote(kv.at[head, OWN], kv.at[head, slot], own_send, own_recv, head, side)

    def relay_copy(head, side):
        slot = OWN + 1 if side == 0 else OWN - 1
        target = OWN + 2 if side == 0 else OWN - 2
        return remote(kv.at[head, slot], kv.at[head, target], relay_send, relay_recv, head, side)

    def far_copy(head, side):
        return remote(
            far_out.at[head, side], far_in.at[head, side], far_send, far_recv, head, side
        )

    def near_copy(head, side, which):
        return remote(
            near_out.at[head, side, which],
            near_in.at[head, side, which],
            near_send.at[which],
            near_recv.at[which],
            head,
            side,
        )

    def grad_rows(owner):
        return g_buf.at[:, pl.ds(pl.multiple_of(owner * part, part), part), :]

    def grad_lanes(owner):
        return g_hbm.at[:, :, pl.ds(pl.multiple_of(owner * width, width), width)]

    def grad_chip():
        peer = pair * 2 + 1 - core
        return pltpu.make_async_remote_copy(
            src_ref=grad_lanes(peer),
            dst_ref=grad_rows(group),
            send_sem=chip_send,
            recv_sem=chip_recv,
            device_id=(here, peer),
            device_id_type=MESH,
        )

    def grad_cross(other):
        peer = (1 - pair) * 2 + other
        return pltpu.make_async_remote_copy(
            src_ref=grad_lanes(peer),
            dst_ref=grad_rows(group),
            send_sem=cross_send.at[other],
            recv_sem=cross_recv.at[core],
            device_id=(here, peer),
            device_id_type=MESH,
        )

    def grad_half(other):
        return pltpu.make_async_remote_copy(
            src_ref=grad_lanes((1 - pair) * 2 + other),
            dst_ref=g_mid.at[other],
            send_sem=half_send.at[other],
            recv_sem=half_recv.at[other],
            device_id=(partner, next_pair * 2 + core),
            device_id_type=MESH,
        )

    def grad_onward(other):
        return pltpu.make_async_remote_copy(
            src_ref=g_mid.at[other],
            dst_ref=grad_rows((1 - next_pair) * 2 + core),
            send_sem=cross_send.at[other],
            recv_sem=cross_recv.at[core],
            device_id=(partner, next_pair * 2 + other),
            device_id_type=MESH,
        )

    def grad_arrival(other):
        return pltpu.make_async_remote_copy(
            src_ref=g_mid.at[other],
            dst_ref=grad_rows((1 - pair) * 2 + other),
            send_sem=cross_send.at[other],
            recv_sem=cross_recv.at[other],
            device_id=(here, (1 - pair) * 2 + other),
            device_id_type=MESH,
        )

    def grad_here():
        return pltpu.make_async_copy(grad_lanes(group), grad_rows(group), g_here)


    barrier = pltpu.get_barrier_semaphore()
    for neighbour in toward:
        pl.semaphore_signal(barrier, inc=1, device_id=(neighbour, group), device_id_type=MESH)
    for step in range(1, groups):
        pl.semaphore_signal(
            barrier,
            inc=1,
            device_id=(here, lax.rem(group + step, groups)),
            device_id_type=MESH,
        )

    @pl.when(special)
    def _():
        for peer in range(groups):
            pl.semaphore_signal(barrier, inc=1, device_id=(partner, peer), device_id_type=MESH)

    for which in range(2):
        load(which, 0).start()
    pl.semaphore_wait(barrier, 2 + groups - 1 + jnp.where(special, groups, 0))

    def send_own(head):
        load(0, head).wait()
        load(1, head).wait()
        for side in range(2):
            own_copy(head, side).start()

    def send_relay(head):
        for side in (1, 0):
            own_copy(head, side).wait_recv()
            relay_copy(head, side).start()

    send_own(0)
    for which in range(2):
        load(which, 1).start()
    grad_chip().start()

    @pl.when(special)
    def _():
        for other in range(2):
            grad_half(other).start()

    @pl.when(jnp.logical_not(special))
    def _():
        for other in range(2):
            grad_cross(other).start()

    send_own(1)
    for head in range(heads):
        for which in range(3):
            if which == 2 or head > 1:
                load(which, head).start()
    grad_here().start()

    zero_block = jnp.zeros(kv.shape[2:], BF16)
    for empty, side, slots in ((here == 0, 1, (0, 1)), (here == count - 1, 0, (3, 4))):

        @pl.when(empty)
        def _():
            def clear(head, carry):
                for slot in slots:
                    kv[head, slot] = zero_block
                far_in[head, side] = zero_block
                near_in[head, side] = zero_block
                return carry

            lax.fori_loop(0, heads, clear, 0)

    @pl.when(special)
    def _():
        for other in range(2):
            grad_half(other).wait_recv()
            grad_onward(other).start()

    zero_tile = jnp.zeros((tile, tile), BF16)
    for t in range(times):
        for j in range(times):
            w_buf[t, WIN, j] = zero_tile
            ds_buf[t, WIN, j] = zero_tile
    row = lax.broadcasted_iota(jnp.int32, (tile, tile), 0)

    send_relay(0)
    if heads > 2:
        send_own(2)
    send_relay(1)
    for head in range(3, heads):
        send_own(head)

    def tile_step(head, t):
        start = jnp.clip(start_ref[t, here], 0, count - WIN)
        rel = jnp.clip(start - here + OWN, 0, OWN)
        q = q_buf[head, t]
        g = g_buf[t, :, lanes(head)]

        def place(i):
            return i // times, i % times

        def scores(i, top):
            s, j = place(i)
            block = dot_nt(k_cur[rel + s, j], q) * (SCALE * LOG2E)
            block = jnp.where(row < count_ref[j, start + s], block, -jnp.inf)
            s_buf[i] = block
            return jnp.maximum(top, fold(block, jnp.max))

        top = looped(9, chunks, scores, jnp.full((8, tile), -jnp.inf, F32))
        top = jnp.max(top, axis=0, keepdims=True)

        def exps(i, total):
            s, j = place(i)
            block = jnp.exp2(s_buf[i] - top)
            s_buf[i] = block
            dp_buf[i] = dot_nt(v_cur[rel + s, j], g)
            return total + fold(block, jnp.sum)

        total = looped(9, chunks, exps, jnp.zeros((8, tile), F32))
        inverse = 1.0 / jnp.sum(total, axis=0, keepdims=True)

        def attend(i, att):
            s, j = place(i)
            probs = s_buf[i] * inverse
            s_buf[i] = probs
            weights = probs.astype(BF16)
            w_buf[t, s, j] = weights
            return att + dot_nn(vt_cur[rel + s, j], weights)

        att = looped(9, chunks, attend, jnp.zeros((DH, tile), F32))
        rounded = att.astype(BF16).astype(F32)
        att_ref[t, :, lanes(head)] = rounded.T.astype(BF16)
        delta = jnp.sum(g.astype(F32).T * rounded, axis=0, keepdims=True)

        def back(i, dq):
            s, j = place(i)
            dscores = (s_buf[i] * (dp_buf[i] - delta)).astype(BF16)
            ds_buf[t, s, j] = dscores
            return dq + dot_nn(kt_cur[rel + s, j], dscores)

        dq = looped(9, chunks, back, jnp.zeros((DH, tile), F32))
        dq_ref[t, :, lanes(head)] = (dq * SCALE).T.astype(BF16)

    def key_side(head):
        rels = [jnp.clip(start_ref[t, here] - here + OWN, 0, OWN) for t in range(times)]

        def parts(slot, j):
            dk = jnp.zeros((tile, DH), F32)
            dv = jnp.zeros((tile, DH), F32)
            for t in range(times):
                s = slot - rels[t]
                s = jnp.where((s >= 0) & (s < WIN), s, WIN)
                dk = dk + dot_nn(ds_buf[t, s, j], q_buf[head, t])
                dv = dv + dot_nn(w_buf[t, s, j], g_buf[t, :, lanes(head)])
            return dk * SCALE, dv

        for slot in (0, SLOTS - 1, 1, SLOTS - 2, OWN):

            def one(j, carry, slot=slot):
                pair = parts(slot, j)
                for which in range(2):
                    if slot == 0:
                        far_out[head, 0, which, j] = pair[which].astype(BF16)
                    elif slot == SLOTS - 1:
                        far_out[head, 1, which, j] = pair[which].astype(BF16)
                    elif slot == OWN:
                        own_sum[head, which, j] = pair[which]
                    else:
                        near_sum[head, 0 if slot < OWN else 1, which, j] = pair[which]
                return carry

            lax.fori_loop(0, times, one, 0, unroll=True)
            if slot in (0, SLOTS - 1):
                side = 0 if slot == 0 else 1

                @pl.when(head > 0)
                def _():
                    far_copy(head, side).start()

    def send_near(head):
        for side in range(2):
            far_copy(head, side).wait_recv()
            for which in range(2):

                def one(j, carry, which=which, side=side):
                    near_out[head, side, which, j] = (
                        near_sum[head, side, which, j]
                        + far_in[head, side, which, j].astype(F32)
                    ).astype(BF16)
                    return carry

                lax.fori_loop(0, times, one, 0)
                near_copy(head, side, which).start()

    def finish(head):
        for which, out in enumerate((dk_ref, dv_ref)):
            for side in range(2):
                near_copy(head, side, which).wait_recv()

            def one(j, carry, which=which, out=out):
                out[j, :, lanes(head)] = (
                    own_sum[head, which, j]
                    + near_in[head, 0, which, j].astype(F32)
                    + near_in[head, 1, which, j].astype(F32)
                ).astype(BF16)
                return carry

            lax.fori_loop(0, times, one, 0)

    def head_step(head, carry):
        load(2, head).wait()

        @pl.when(head == 0)
        def _():
            grad_here().wait()
            grad_chip().wait_recv()
            for other in range(2):
                grad_arrival(other).wait_recv()

        for side in range(2):
            relay_copy(head, side).wait_recv()

        def stage(i, inner):
            slot, j = i // times, i % times
            keys = kv[head, slot, 0, j]
            values = kv[head, slot, 1, j]
            k_cur[slot, j] = keys
            v_cur[slot, j] = values
            kt_cur[slot, j] = keys.T
            vt_cur[slot, j] = values.T
            return inner

        lax.fori_loop(0, SLOTS * times, stage, 0)

        def visit(t, inner):
            tile_step(head, t)

            @pl.when((head == 0) & (t == 1))
            def _():
                send_relay(2)

            @pl.when((head == 1) & (t == 1))
            def _():
                send_relay(3)
                for side in range(2):
                    far_copy(0, side).start()

            return inner

        lax.fori_loop(0, times, visit, 0)
        key_side(head)

        @pl.when(head > 1)
        def _():
            send_near(head - 2)

        return carry

    lax.fori_loop(0, heads, head_step, 0)
    for head in range(heads - 2, heads):
        send_near(head)
    for head in range(heads - 1):
        finish(head)

    def drain(head, carry):
        for side in range(2):
            own_copy(head, side).wait_send()
            relay_copy(head, side).wait_send()
            far_copy(head, side).wait_send()
        return carry

    def drain_near(head, carry):
        for side in range(2):
            for which in range(2):
                near_copy(head, side, which).wait_send()
        return carry

    lax.fori_loop(0, heads, drain, 0)
    lax.fori_loop(0, heads - 1, drain_near, 0)
    grad_chip().wait_send()
    for other in range(2):
        grad_arrival(other).wait_send()

    @pl.when(special)
    def _():
        for other in range(2):
            grad_half(other).wait_send()

    finish(heads - 1)
    drain_near(heads - 1, 0)


def forward(*refs):
    sources, targets, sems = refs[:4], refs[4:8], refs[8]
    copies = [
        pltpu.make_async_copy(sources[i], targets[i], sems.at[i]) for i in range(4)
    ]
    for copy in copies:
        copy.start()
    for copy in copies:
        copy.wait()


def shards(queries, keys, values, grad_out, window_start, key_counts):
    _, times, tile, width = queries.shape
    heads = width // DH
    groups = tile // grad_out.shape[2]
    block = (times, tile, DH)
    dma = pltpu.SemaphoreType.DMA
    any_spec = pl.BlockSpec(memory_space=pl.ANY)
    vmem_spec = pl.BlockSpec(memory_space=pltpu.VMEM)
    smem_spec = pl.BlockSpec(memory_space=pltpu.SMEM)
    out = jax.ShapeDtypeStruct((times, tile, width), BF16)
    pairs = times * heads * 6 * tile * WIN * times * tile * DH * 2
    results = pl.pallas_call(
        functools.partial(kernel, heads, times, tile, groups),
        out_shape=(pltpu.VMEM(out.shape, BF16),) * 4,
        in_specs=[smem_spec, smem_spec] + [any_spec] * 4,
        out_specs=(vmem_spec,) * 4,
        scratch_shapes=[
            pltpu.VMEM((heads, SLOTS, 2) + block, BF16),
            pltpu.VMEM((heads, 2, 2) + block, BF16),
            pltpu.VMEM((heads, 2, 2) + block, BF16),
            pltpu.VMEM((heads, 2, 2) + block, BF16),
            pltpu.VMEM((heads, 2, 2) + block, BF16),
            pltpu.VMEM((heads, 2, 2) + block, F32),
            pltpu.VMEM((heads, 2) + block, F32),
            pltpu.VMEM((heads,) + block, BF16),
            pltpu.VMEM((times, tile, width), BF16),
            pltpu.VMEM((SLOTS, times, tile, DH), BF16),
            pltpu.VMEM((SLOTS, times, tile, DH), BF16),
            pltpu.VMEM((SLOTS, times, DH, tile), BF16),
            pltpu.VMEM((SLOTS, times, DH, tile), BF16),
            pltpu.VMEM((WIN * times, tile, tile), F32),
            pltpu.VMEM((WIN * times, tile, tile), F32),
            pltpu.VMEM((times, WIN + 1, times, tile, tile), BF16),
            pltpu.VMEM((times, WIN + 1, times, tile, tile), BF16),
            dma((heads, 3)),
            dma,
            dma,
            dma,
            dma((2,)),
            dma((2,)),
            dma((2,)),
            dma((2,)),
            pltpu.VMEM((2, times, tile // groups, width), BF16),
            dma((heads, 2)),
            dma((heads, 2)),
            dma((heads, 2)),
            dma((heads, 2)),
            dma((heads, 2)),
            dma((heads, 2)),
            dma((2, heads, 2)),
            dma((2, heads, 2)),
        ],
        compiler_params=pltpu.CompilerParams(
            collective_id=0, has_side_effects=True, vmem_limit_bytes=54 * 1024 * 1024
        ),
        cost_estimate=pl.CostEstimate(
            flops=pairs, bytes_accessed=8 * times * tile * width * 2, transcendentals=0
        ),
        name="band_attention",
    )(window_start.T, key_counts.T, queries[0], keys[0], values[0], grad_out[0])
    results = pl.pallas_call(
        forward,
        out_shape=(out,) * 4,
        in_specs=[vmem_spec] * 4,
        out_specs=(any_spec,) * 4,
        scratch_shapes=[dma((4,))],
        compiler_params=pltpu.CompilerParams(vmem_limit_bytes=4 * 1024 * 1024),
        name="place_results",
    )(*results)
    return tuple(result[None] for result in results)


def solution(mesh):
    placed = (
        P("ctx", None, None, "head"),
        P("ctx", None, None, "head"),
        P("ctx", None, None, "head"),
        P("ctx", None, "head", None),
        P(),
        P(),
    )
    return jax.shard_map(
        shards,
        mesh=mesh,
        in_specs=placed,
        out_specs=(P("ctx", None, None, "head"),) * 4,
        check_vma=False,
    )
```
